128 devices in a mesh: word: 16 (over y, x), ctx: 8 (over z, core).
Axes of the slice: x: 4, y: 4, z: 4, core: 2. Of those that a mesh axis runs over, the one named last changes fastest.
Arguments:
- counts: int32 [16384, 16384], P('word', 'ctx'), may hold values from 0 to 80, as said below
- row_totals: int32 [16384], P('word'), may hold values from 16384 to 262143
- ctx_totals: int32 [16384], P('ctx'), may hold values from 16384 to 262143
- samples: int32 [2048], replicated, may hold values from 0 to 16383, as said below
Outputs:
- factor: float32 [16384, 2048], P(('word', 'ctx'))
The draws below stay inside these ranges and needn't reach their ends.
Inputs may be any that keep to these rules, and one draw needn't show every extreme that they name: symmetric: counts[i, j] equals counts[j, i]. `samples`: distinct words; among the 1024 words of one index of word at most 256 are sampled, and some such block holds exactly 256.
All inputs are finite; a program needn't handle non-finite values.
Results may differ from the reference program's by a relative error of at most 0.0035.
Values may be sent and summed in bfloat16 or wider, within the bound.
No kernel may reach another device: no remote copies, remote signals or barrier semaphores. Data moves between devices by JAX's collectives and lax.ppermute only.
A program may use at most 192 MiB of HBM per device.

```python
import math
import jax
import jax.numpy as jnp
from jax import lax

ROWS_DEV = 1024
SAMPLES = 2048
VOCAB = 16384


def draw_counts(key, part):
    key = jax.random.fold_in(key, 5)
    raw = jax.random.randint(key, (VOCAB, VOCAB), 0, 64)
    half = jnp.where(raw < 24, 0, raw - 23)
    return (half + half.T).astype(jnp.int32)


def draw_samples(key, part):
    key = jax.random.fold_in(key, 11)
    key_hot, key_jitter, key_rank, key_order = jax.random.split(key, 4)
    blocks = VOCAB // ROWS_DEV
    most = 2 * SAMPLES // blocks
    rest = SAMPLES - most
    base = rest // (blocks - 1)
    extra = rest - base * (blocks - 1)
    hot = jax.random.randint(key_hot, (), 0, blocks)
    others = jnp.arange(blocks - 1, dtype=jnp.int32)
    jitter = jax.random.randint(key_jitter, (blocks - 1,), 0, base // 2 + 1)
    loads = base + (others < extra).astype(jnp.int32) + jitter - jnp.roll(jitter, 1)
    block_ids = jnp.arange(blocks, dtype=jnp.int32)
    shifted = jnp.clip(block_ids - (block_ids > hot).astype(jnp.int32), 0, blocks - 2)
    full = jnp.where(block_ids == hot, most, jnp.take(loads, shifted))
    scores = jax.random.randint(key_rank, (blocks, ROWS_DEV), 0, 2 ** 16) * ROWS_DEV + jnp.arange(ROWS_DEV, dtype=jnp.int32)[None, :]
    ranks = jnp.argsort(jnp.argsort(scores, axis=1), axis=1)
    chosen = (ranks < full[:, None]).reshape(-1)
    order_key = jax.random.randint(key_order, (VOCAB,), 0, 2 ** 15) * VOCAB + jnp.arange(VOCAB, dtype=jnp.int32)
    order_key = jnp.where(chosen, order_key, -1)
    values, picked = lax.top_k(order_key, SAMPLES)
    return picked.astype(jnp.int32)


def with_ends(values, key, low, largest):
    longest = values.shape.index(max(values.shape))
    spots = []
    for shift in (0, 1):
        where = [jax.random.randint(jax.random.fold_in(key, axis), (), 0, length) for axis, length in enumerate(values.shape)]
        where[longest] = (where[longest] + shift) % values.shape[longest]
        spots.append(tuple(where))
    return values.at[spots[0]].set(low).at[spots[1]].set(largest)


def setup_inputs(seed: int = 0) -> dict:
    keys = jax.random.split(jax.random.key(seed), 5)
    counts = draw_counts(jax.random.fold_in(keys[4], 71), 0)
    row_totals = with_ends(jax.random.randint(keys[1], (VOCAB,), VOCAB, 16 * VOCAB), jax.random.fold_in(keys[1], 1), VOCAB, (16 * VOCAB) - 1).astype(jnp.int32)
    ctx_totals = with_ends(jax.random.randint(keys[2], (VOCAB,), VOCAB, 16 * VOCAB), jax.random.fold_in(keys[2], 1), VOCAB, (16 * VOCAB) - 1).astype(jnp.int32)
    samples = draw_samples(jax.random.fold_in(keys[4], 71), 0)
    return dict(counts=counts, row_totals=row_totals, ctx_totals=ctx_totals, samples=samples)


NEG_LOG = math.log(5.0)

def ppmi(count, log_total, row_log, col_log):
    counted = jnp.maximum(count, 1).astype(jnp.float32)
    value = jnp.log(counted) + log_total - row_log[:, None] - col_log[None, :] - NEG_LOG
    return jnp.where(count > 0, jnp.maximum(value, 0.0), 0.0).astype(jnp.bfloat16)

def highest_dot(left, right):
    return jnp.dot(left.astype(jnp.float32), right.astype(jnp.float32), precision=lax.Precision.HIGHEST, preferred_element_type=jnp.float32)

def blocked_factor(core, rows):
    total = core.shape[0]
    width = min(512, total)
    count = total // width
    lowers = {}
    inverses = []
    for j in range(count):
        for i in range(j, count):
            accum = core[i * width:(i + 1) * width, j * width:(j + 1) * width]
            for k in range(j):
                accum = accum - highest_dot(lowers[i, k], lowers[j, k].T)
            if i == j:
                diag_low = jnp.linalg.cholesky(accum)
                eye_block = jnp.eye(width, dtype=jnp.float32)
                inverses.append(jax.scipy.linalg.solve_triangular(diag_low, eye_block, lower=True))
                lowers[j, j] = diag_low
            else:
                lowers[i, j] = highest_dot(accum, inverses[j].T)
    pieces = []
    for j in range(count):
        accum = rows[:, j * width:(j + 1) * width]
        for k in range(j):
            accum = accum - highest_dot(pieces[k], lowers[j, k].T)
        pieces.append(highest_dot(accum, inverses[j].T))
    return jnp.concatenate(pieces, axis=1)

def reference(counts, row_totals, ctx_totals, samples):
    row_float = row_totals.astype(jnp.float32)
    ctx_float = ctx_totals.astype(jnp.float32)
    log_total = jnp.log(jnp.sum(row_float))
    weight_log = 0.5 * (jnp.log(row_float) + jnp.log(ctx_float))
    picked = jnp.take(counts, samples, axis=1)
    columns = ppmi(picked, log_total, weight_log, jnp.take(weight_log, samples))
    shift = 4.0 * math.sqrt(SAMPLES)
    core = jnp.take(columns, samples, axis=0).astype(jnp.float32) + shift * jnp.eye(SAMPLES, dtype=jnp.float32)
    return blocked_factor(core, columns.astype(jnp.float32))
```

```python
import math

import jax
import jax.numpy as jnp
from jax import lax
from jax.experimental import pallas as pl
from jax.experimental.pallas import tpu as pltpu
from jax.sharding import PartitionSpec as P

SAMPLES = 2048


NEG_LOG = math.log(5.0)


def ppmi(count, log_total, row_log, col_log):
    counted = jnp.maximum(count, 1).astype(jnp.float32)
    value = jnp.log(counted) + log_total - row_log[:, None] - col_log[None, :] - NEG_LOG
    return jnp.where(count > 0, jnp.maximum(value, 0.0), 0.0).astype(jnp.bfloat16)


def highest_dot(left, right):
    return jnp.dot(left, right, precision=lax.Precision.HIGHEST, preferred_element_type=jnp.float32)


def blocked_factor(core, rows):
    total = core.shape[0]
    width = min(512, total)
    count = total // width
    lowers = {}
    inverses = []
    for j in range(count):
        for i in range(j, count):
            accum = core[i * width : (i + 1) * width, j * width : (j + 1) * width]
            for k in range(j):
                accum = accum - highest_dot(lowers[i, k], lowers[j, k].T)
            if i == j:
                diag_low = jnp.linalg.cholesky(accum)
                eye_block = jnp.eye(width, dtype=jnp.float32)
                inverses.append(jax.scipy.linalg.solve_triangular(diag_low, eye_block, lower=True))
                lowers[j, j] = diag_low
            else:
                lowers[i, j] = highest_dot(accum, inverses[j].T)
    pieces = []
    for j in range(count):
        accum = rows[:, j * width : (j + 1) * width]
        for k in range(j):
            accum = accum - highest_dot(pieces[k], lowers[j, k].T)
        pieces.append(highest_dot(accum, inverses[j].T))
    return jnp.concatenate(pieces, axis=1)


BLOCK = 256
SHIFT = 4.0 * math.sqrt(SAMPLES)
TOLERANCE = 1e-3
ROUNDS = (3, 2, 2, 2, 2, 2, 3, 4)


def dot_nn(left, right):
    return lax.dot_general(left, right, (((1,), (0,)), ((), ())), preferred_element_type=jnp.float32)


def dot_nt(left, right):
    return lax.dot_general(left, right, (((1,), (1,)), ((), ())), preferred_element_type=jnp.float32)


def factor_kernel(core_ref, own_ref, out_ref, worst_ref, low_ref):
    total = core_ref.shape[0]
    out_rows = own_ref.shape[0]
    half = jnp.bfloat16
    row_id = lax.broadcasted_iota(jnp.int32, (BLOCK, BLOCK), 0)
    col_id = lax.broadcasted_iota(jnp.int32, (BLOCK, BLOCK), 1)
    diag = row_id == col_id
    below = row_id > col_id
    weight = jnp.where(below, 1.0, jnp.where(diag, 0.5, 0.0))
    worst = jnp.zeros((1, 1), jnp.float32)
    for k in range(total // BLOCK):
        lo, hi = k * BLOCK, (k + 1) * BLOCK
        block = core_ref[lo:hi, lo:hi].astype(jnp.float32)
        if k:
            pivot = low_ref[lo:hi, :lo]
            block = block - dot_nt(pivot, pivot)
        on_diag = jnp.where(diag, block + SHIFT, 0.0)
        scale_col = lax.rsqrt(jnp.sum(on_diag, axis=1, keepdims=True))
        scale_row = lax.rsqrt(jnp.sum(on_diag, axis=0, keepdims=True))
        off = jnp.where(diag, 0.0, block * scale_col * scale_row)
        off_half = off.astype(half)
        inv = jnp.where(below, -off, 0.0)
        for _ in range(ROUNDS[k]):
            inv_half = inv.astype(half)
            inner = off + dot_nn(inv_half, off_half)
            resid = inner + dot_nt((inner + inv).astype(half), inv_half)
            step = inv + resid * weight
            inv = inv - step - dot_nn(step.astype(half), inv_half)
        worst = jnp.maximum(worst, jnp.sum(step * step, keepdims=True))
        inv_half = inv.astype(half)
        if hi < total:
            under = core_ref[hi:, lo:hi].astype(jnp.float32)
            if k:
                under = under - dot_nt(low_ref[hi:total, :lo], pivot)
            under = under * scale_row
            low_ref[hi:total, lo:hi] = (under + dot_nt(under.astype(half), inv_half)).astype(half)
        mine = own_ref[:, lo:hi].astype(jnp.float32)
        if k:
            mine = mine - dot_nt(low_ref[total:, :lo], pivot)
        mine = mine * scale_row
        mine = mine + dot_nt(mine.astype(half), inv_half)
        out_ref[:, lo:hi] = mine
        low_ref[total:, lo:hi] = mine.astype(half)
    worst_ref[...] = jnp.broadcast_to(worst, worst_ref.shape)


def fast_factor(core, own):
    total, out_rows = core.shape[0], own.shape[0]
    vmem = pl.BlockSpec(memory_space=pltpu.VMEM)
    return pl.pallas_call(
        factor_kernel,
        out_shape=(
            jax.ShapeDtypeStruct((out_rows, total), jnp.float32),
            jax.ShapeDtypeStruct((8, 128), jnp.float32),
        ),
        in_specs=[vmem, vmem],
        out_specs=(vmem, vmem),
        scratch_shapes=[pltpu.VMEM((total + out_rows, total), jnp.bfloat16)],
        compiler_params=pltpu.CompilerParams(vmem_limit_bytes=56 * 1024 * 1024),
    )(core, own)


def robust_factor(core, own):
    n = core.shape[0]
    shifted = core.astype(jnp.float32) + SHIFT * jnp.eye(n, dtype=jnp.float32)
    return blocked_factor(shifted, own.astype(jnp.float32))


def factor(core, own):
    out, worst = fast_factor(core, own)
    return lax.cond(
        worst[0, 0] < TOLERANCE, lambda c, o, r: r, lambda c, o, r: robust_factor(c, o), core, own, out
    )


def owner_slots(owner, local_index, position, owners, capacity):
    labels = jnp.arange(owners, dtype=jnp.int32)
    member = (owner[:, None] == labels[None, :]).astype(jnp.int32)
    rank = jnp.sum((jnp.cumsum(member, axis=0) - 1) * member, axis=1)
    target = jnp.where(owner == position, rank, capacity)
    slot_index = jnp.zeros((capacity,), jnp.int32).at[target].set(local_index, mode="drop")
    return (rank, slot_index)


def body(counts, row_totals, ctx_totals, samples):
    rows_dev, ctx_dev = counts.shape
    n_word = lax.axis_size("word")
    n_ctx = lax.axis_size("ctx")
    word_pos = lax.axis_index("word")
    ctx_pos = lax.axis_index("ctx")
    n_samples = samples.shape[0]
    col_width = n_samples // n_ctx
    out_rows = rows_dev // n_ctx
    cap_rows = 2 * n_samples // n_word
    cap_cols = cap_rows * (n_word // n_ctx)
    every_row = lax.all_gather(row_totals, "word", axis=0, tiled=True).astype(jnp.float32)
    every_ctx = lax.all_gather(ctx_totals, "ctx", axis=0, tiled=True).astype(jnp.float32)
    log_total = jnp.log(jnp.sum(every_row))
    weight_log = 0.5 * (jnp.log(every_row) + jnp.log(every_ctx))
    row_log = lax.dynamic_slice_in_dim(weight_log, word_pos * rows_dev, rows_dev)
    col_owner = samples // ctx_dev
    local_col = samples - col_owner * ctx_dev
    col_rank, slot_col = owner_slots(col_owner, local_col, ctx_pos, n_ctx, cap_cols)
    picked = jnp.take(counts, slot_col, axis=1)
    block = ppmi(picked, log_total, row_log, jnp.take(weight_log, ctx_pos * ctx_dev + slot_col))
    col_slot = col_owner * cap_cols + col_rank
    row_owner = samples // rows_dev
    local_row = samples - row_owner * rows_dev
    row_rank, slot_row = owner_slots(row_owner, local_row, word_pos, n_word, cap_rows)
    gathered = lax.all_gather(block, "ctx", axis=1, tiled=True)
    columns = jnp.take(gathered, col_slot, axis=1)
    own_rows = lax.dynamic_slice_in_dim(columns, ctx_pos * out_rows, out_rows, 0)
    col_part = lax.dynamic_slice_in_dim(columns, ctx_pos * col_width, col_width, 1)
    piece = jnp.take(col_part, slot_row, axis=0)
    core_slot = row_owner * cap_rows + row_rank
    wide = lax.all_gather(piece, "ctx", axis=1, tiled=True)
    stacked = lax.all_gather(wide, "word", axis=0, tiled=True)
    core = jnp.take(stacked, core_slot, axis=0)
    return factor(core, own_rows)


def solution(mesh):
    placed = (P("word", "ctx"), P("word"), P("ctx"), P())
    return jax.shard_map(
        body, mesh=mesh, in_specs=placed, out_specs=P(("word", "ctx"), None), check_vma=False
    )
```

```python
import math

import jax
import jax.numpy as jnp
from jax import lax
from jax.experimental import pallas as pl
from jax.experimental.pallas import tpu as pltpu
from jax.sharding import PartitionSpec as P

SAMPLES = 2048


NEG_LOG = math.log(5.0)


def highest_dot(left, right):
    return jnp.dot(left, right, precision=lax.Precision.HIGHEST, preferred_element_type=jnp.float32)


def blocked_factor(core, rows):
    total = core.shape[0]
    width = min(512, total)
    count = total // width
    lowers = {}
    inverses = []
    for j in range(count):
        for i in range(j, count):
            accum = core[i * width : (i + 1) * width, j * width : (j + 1) * width]
            for k in range(j):
                accum = accum - highest_dot(lowers[i, k], lowers[j, k].T)
            if i == j:
                diag_low = jnp.linalg.cholesky(accum)
                eye_block = jnp.eye(width, dtype=jnp.float32)
                inverses.append(jax.scipy.linalg.solve_triangular(diag_low, eye_block, lower=True))
                lowers[j, j] = diag_low
            else:
                lowers[i, j] = highest_dot(accum, inverses[j].T)
    pieces = []
    for j in range(count):
        accum = rows[:, j * width : (j + 1) * width]
        for k in range(j):
            accum = accum - highest_dot(pieces[k], lowers[j, k].T)
        pieces.append(highest_dot(accum, inverses[j].T))
    return jnp.concatenate(pieces, axis=1)


BLOCK = 256
SHIFT = 4.0 * math.sqrt(SAMPLES)
TOLERANCE = 1e-3
ROUNDS = (3, 2, 2, 2, 2, 2, 3, 4)


def dot_nn(left, right):
    return lax.dot_general(left, right, (((1,), (0,)), ((), ())), preferred_element_type=jnp.float32)


def dot_nt(left, right):
    return lax.dot_general(left, right, (((1,), (1,)), ((), ())), preferred_element_type=jnp.float32)


def place_parts(refs, ctx, all_ref):
    for source, parts in sources(refs, ctx):
        lanes = pl.ds(pl.multiple_of(source * 128, 128), 128)
        start = 0
        for part in parts:
            all_ref[start : start + part.shape[0], lanes] = part[...]
            start += part.shape[0]


def factor_kernel(pos_ref, stat_ref, own_ref, *refs):
    part_refs, (out_ref, worst_ref, all_ref, core_ref, low_ref) = refs[:10], refs[10:]
    total = core_ref.shape[0]
    middle = total // 2
    half = jnp.bfloat16
    place_parts(part_refs, pos_ref[1], all_ref)
    row_id = iota((BLOCK, BLOCK), 0)
    col_id = iota((BLOCK, BLOCK), 1)
    diag = row_id == col_id
    below = row_id > col_id
    above = row_id < col_id
    eye = one_hot(diag)
    zero = jnp.zeros((BLOCK, BLOCK), half)

    def turned(tile):
        return dot_nt(eye, tile).astype(half)

    count = middle // BLOCK
    for i in range(count):
        for side in (0, middle):
            here = slice(side + i * BLOCK, side + (i + 1) * BLOCK)
            for j in range(i):
                core_ref[here, side + j * BLOCK : side + (j + 1) * BLOCK] = turned(
                    all_ref[side + j * BLOCK : side + (j + 1) * BLOCK, i * BLOCK : (i + 1) * BLOCK]
                )
            upper = jnp.where(above, all_ref[here, i * BLOCK : (i + 1) * BLOCK], zero)
            core_ref[here, here] = upper + turned(upper)
        here = slice(middle + i * BLOCK, middle + (i + 1) * BLOCK)
        for j in range(count):
            cols = slice(j * BLOCK, (j + 1) * BLOCK)
            if i > j:
                tile = all_ref[here, cols]
            else:
                tile = turned(all_ref[cols, i * BLOCK : (i + 1) * BLOCK])
            if i == j:
                tile = jnp.where(above, tile, all_ref[here, cols])
            core_ref[here, cols] = tile

    weight = jnp.where(below, 1.0, jnp.where(diag, 0.5, 0.0))
    worst = jnp.zeros((1, 1), jnp.float32)
    for k in range(total // BLOCK):
        lo, hi = k * BLOCK, (k + 1) * BLOCK
        block = core_ref[lo:hi, lo:hi].astype(jnp.float32)
        block = jnp.where(diag, stat_ref[1:2, lo:hi] + SHIFT, block)
        if k:
            pivot = low_ref[lo:hi, :lo]
            block = block - dot_nt(pivot, pivot)
        on_diag = jnp.where(diag, block, 0.0)
        scale_col = lax.rsqrt(jnp.sum(on_diag, axis=1, keepdims=True))
        scale_row = lax.rsqrt(jnp.sum(on_diag, axis=0, keepdims=True))
        off = jnp.where(diag, 0.0, block * scale_col * scale_row)
        off_half = off.astype(half)
        inv = jnp.where(below, -off, 0.0)
        for _ in range(ROUNDS[k]):
            inv_half = inv.astype(half)
            inner = off + dot_nn(inv_half, off_half)
            resid = inner + dot_nt((inner + inv).astype(half), inv_half)
            step = inv + resid * weight
            inv = inv - step - dot_nn(step.astype(half), inv_half)
        worst = jnp.maximum(worst, jnp.sum(step * step, keepdims=True))
        inv_half = inv.astype(half)
        if hi < total:
            under = core_ref[hi:, lo:hi].astype(jnp.float32)
            if k:
                under = under - dot_nt(low_ref[hi:total, :lo], pivot)
            under = under * scale_row
            low_ref[hi:total, lo:hi] = (under + dot_nt(under.astype(half), inv_half)).astype(half)
        mine = own_ref[:, lo:hi].astype(jnp.float32)
        if k:
            mine = mine - dot_nt(low_ref[total:, :lo], pivot)
        mine = mine * scale_row
        mine = mine + dot_nt(mine.astype(half), inv_half)
        out_ref[:, lo:hi] = mine
        low_ref[total:, lo:hi] = mine.astype(half)
    worst_ref[...] = jnp.broadcast_to(worst, worst_ref.shape)


def fast_factor(pos, parts, stat, own):
    out_rows, total = own.shape
    vmem = pl.BlockSpec(memory_space=pltpu.VMEM)
    smem = pl.BlockSpec(memory_space=pltpu.SMEM)
    return pl.pallas_call(
        factor_kernel,
        out_shape=(
            jax.ShapeDtypeStruct((out_rows, total), jnp.float32),
            jax.ShapeDtypeStruct((8, 128), jnp.float32),
        ),
        in_specs=[smem] + [vmem] * 12,
        out_specs=(vmem, vmem),
        scratch_shapes=[
            pltpu.VMEM((total, total // 2), jnp.bfloat16),
            pltpu.VMEM((total, total), jnp.bfloat16),
            pltpu.VMEM((total + out_rows, total), jnp.bfloat16),
        ],
        compiler_params=params(56),
    )(pos, stat, own, *parts)


def robust_factor(pos, parts, stat, own):
    total = own.shape[1]
    middle = total // 2
    every = jnp.zeros((total, middle), jnp.float32)
    for source, group in sources(parts, pos[1]):
        block = jnp.concatenate(group, axis=0).astype(jnp.float32)
        every = lax.dynamic_update_slice(every, block, (0, source * 128))
    upper, lower = every[:middle], every[middle:]
    first, second = jnp.triu(upper, 1), jnp.triu(lower, 1)
    cross = jnp.tril(lower) + jnp.tril(upper, -1).T
    core = jnp.block([[first + first.T, cross.T], [cross, second + second.T]])
    core = core + jnp.diag(stat[1] + SHIFT)
    return blocked_factor(core, own.astype(jnp.float32))


def factor(pos, parts, stat, own):
    out, worst = fast_factor(pos, parts, stat, own)
    return lax.cond(
        worst[0, 0] < TOLERANCE,
        lambda p, q, s, o, r: r,
        lambda p, q, s, o, r: robust_factor(p, q, s, o),
        pos, parts, stat, own, out,
    )


SLOTS = 256
EXTRA = 16
TOP = (SLOTS + EXTRA) // 32 * 16 + 16
MEGA = 1024 * 1024


def params(limit=48):
    return pltpu.CompilerParams(vmem_limit_bytes=limit * MEGA)


def iota(shape, dim):
    return lax.broadcasted_iota(jnp.int32, shape, dim)


def to_col(row):
    n = row.shape[1]
    square = iota((n, n), 0) == iota((n, n), 1)
    return jnp.sum(jnp.where(square, jnp.broadcast_to(row, (n, n)), 0.0), axis=1, keepdims=True)


def to_row(col):
    n = col.shape[0]
    square = iota((n, n), 0) == iota((n, n), 1)
    return jnp.sum(jnp.where(square, jnp.broadcast_to(col, (n, n)), 0.0), axis=0, keepdims=True)


def stack_rows(rows, height):
    width = rows[0].shape[1]
    index = iota((height, width), 0)
    out = jnp.zeros((height, width), jnp.float32)
    for r, row in enumerate(rows):
        out = jnp.where(index == r, jnp.broadcast_to(row, (height, width)), out)
    return out


def one_hot(mask):
    return jnp.where(mask, 1.0, 0.0).astype(jnp.bfloat16)


def pieces(value):
    high = value.astype(jnp.bfloat16).astype(jnp.float32)
    rest = value - high
    middle = rest.astype(jnp.bfloat16).astype(jnp.float32)
    return [high, middle, rest - middle]


def byte_pieces(value):
    return [(value >> shift & 255).astype(jnp.float32) for shift in (16, 8, 0)]


def select_kernel(pos_ref, samples_ref, counts_ref, ctx_ref, *refs):
    chunk_refs, (send_ref, slot_ref, index_ref, hot_ref, picked_ref) = refs[:8], refs[8:]
    g = pl.program_id(0)
    word, ctx = pos_ref[0], pos_ref[1]
    n = samples_ref.shape[1]
    rows = counts_ref.shape[0]
    width = hot_ref.shape[1]

    @pl.when(g == 0)
    def _():
        sample = samples_ref[...]
        block = sample >> 10
        member = jnp.where(iota((16, n), 0) == block, 1.0, 0.0)
        before = one_hot(iota((256, 256), 0) < iota((256, 256), 1))
        count = jnp.zeros((16, 1), jnp.float32)
        k = iota((1, n), 1)
        local = sample & 2047
        vals = stack_rows(
            [v.astype(jnp.float32) for v in (local >> 8, local & 255, local * 0 + 1, k >> 8, k & 255, (local & 1023) >> 8)],
            8,
        ).astype(jnp.bfloat16)
        by_ctx = jnp.zeros((8, width), jnp.float32)
        by_word = jnp.zeros((8, SLOTS), jnp.float32)
        for t in range(n // 256):
            cut = slice(256 * t, 256 * t + 256)
            mine = member[:, cut]
            rank = dot_nn(mine.astype(jnp.bfloat16), before) + count
            count = count + jnp.sum(mine, axis=1, keepdims=True)
            slot = block[:, cut].astype(jnp.float32) * SLOTS + jnp.sum(mine * rank, axis=0, keepdims=True)
            slot_ref[:, cut] = slot.astype(jnp.int32)
            column = to_col(slot).astype(jnp.int32)
            by_ctx += dot_nn(vals[:, cut], one_hot(column - ctx * width == iota((256, width), 1)))
            by_word += dot_nn(vals[:, cut], one_hot(column - word * SLOTS == iota((256, SLOTS), 1)))
        col = jnp.where(by_ctx[2:3] > 0, by_ctx[0:1] * 256 + by_ctx[1:2], -1.0).astype(jnp.int32)
        for t in range(hot_ref.shape[0] // 256):
            hot_ref[256 * t : 256 * t + 256] = one_hot(iota((256, width), 0) + 256 * t == col)
        row = jnp.where(by_word[2:3] > 0, by_word[5:6] * 256 + by_word[1:2], -1.0)
        index_ref[...] = stack_rows([row, by_word[3:4] * 256 + by_word[4:5]], 8)

    chunk = dot_nn(counts_ref[...].astype(jnp.float32).astype(jnp.bfloat16), hot_ref[...]).astype(jnp.bfloat16)
    picked_ref[pl.ds(pl.multiple_of(g * rows, rows), rows), :] = chunk
    shift = ((g >> 1) - (ctx >> 1) & 3) * 2 + ((g ^ ctx) & 1)
    for r in range(8):

        @pl.when(shift == r)
        def _(r=r):
            chunk_refs[r][...] = chunk

    @pl.when(g == pl.num_programs(0) - 1)
    def _():
        total_rows = picked_ref.shape[0]
        row_col = to_col(index_ref[0:1]).astype(jnp.int32)
        picked = dot_nn(one_hot(row_col == iota((SLOTS, total_rows), 1)), picked_ref[...])
        odd = (word & 1) == 1
        tile = jnp.where(odd, picked[:, SLOTS:], picked[:, :SLOTS])
        square = iota((SLOTS, SLOTS), 0) == iota((SLOTS, SLOTS), 1)
        own_diag = jnp.sum(jnp.where(square, tile, 0.0), axis=0, keepdims=True)
        here = ctx_ref[:, pl.ds(pl.multiple_of((word & 1) * total_rows, total_rows), total_rows)]
        parts = []
        for piece in byte_pieces(here):
            parts += [piece[:, :width], piece[:, width:]]
        parts.append(jnp.concatenate([own_diag, jnp.zeros_like(own_diag)], axis=1))
        send_ref[:SLOTS] = picked.astype(jnp.bfloat16)
        send_ref[SLOTS:] = stack_rows(parts, EXTRA).astype(jnp.bfloat16)


def sources(refs, ctx):
    z, core = ctx >> 1, ctx & 1
    out = []
    for half in (0, 1):
        own, left, right, top, bottom = refs[5 * half : 5 * half + 5]
        for step, parts in ((0, (own,)), (3, (left,)), (1, (right,)), (2, (top, bottom))):
            out.append((((z + step) & 3) * 2 + (core ^ half), parts))
    return out


def block_kernel(pos_ref, slot_ref, index_ref, totals_ref, *refs):
    in_refs, (send_ref, own_ref, weight_ref) = refs[:10], refs[10:]
    word, ctx = pos_ref[0], pos_ref[1]
    width = in_refs[0].shape[1]
    first = pl.multiple_of(ctx * 128, 128)
    wanted = jnp.concatenate([slot_ref[:, pl.ds(first, 128)], slot_ref[:, pl.ds(first + 1024, 128)]], axis=1)
    acc = jnp.zeros((SLOTS, 256), jnp.float32)
    extra = jnp.zeros((EXTRA, width), jnp.float32)
    for source, parts in sources(in_refs, ctx):
        hot = one_hot(iota((width, 256), 0) + source * width == wanted)
        found = [dot_nn(part[...], hot) for part in parts]
        if len(parts) == 2:
            found = jnp.concatenate([found[0], found[1][: SLOTS - TOP]], axis=0)
        else:
            found = found[0][:SLOTS]
        acc += found
        last = parts[-1].shape[0] - EXTRA
        extra += jnp.where(source == word >> 1, parts[-1][last:].astype(jnp.float32), 0.0)
    ctx_total = [jnp.concatenate([extra[2 * p : 2 * p + 1], extra[2 * p + 1 : 2 * p + 2]], axis=1) for p in range(3)]
    ctx_total = ctx_total[0] * 65536.0 + ctx_total[1] * 256.0 + ctx_total[2]
    row_total = totals_ref[...].astype(jnp.float32)
    weight = 0.5 * (jnp.log(row_total) + jnp.log(ctx_total))
    weight_ref[...] = jnp.broadcast_to(weight, weight_ref.shape)
    own_ref[...] = weight_ref[:, pl.ds(first, 128)]
    row_col = to_col(index_ref[0:1]).astype(jnp.int32)
    hot = one_hot(row_col == iota((SLOTS, weight.shape[1]), 1))
    slot_weight = dot_nt(stack_rows(pieces(weight), 16).astype(jnp.bfloat16), hot)
    total = [jnp.broadcast_to(p, (1, 128)) for p in pieces(jnp.sum(row_total, axis=1, keepdims=True))]
    parts = []
    for p in range(3):
        parts += [slot_weight[p : p + 1, :128], slot_weight[p : p + 1, 128:]]
    parts += [extra[6:7, :128], extra[6:7, 128:256]] + total
    tail = stack_rows(parts, EXTRA).astype(jnp.bfloat16)
    k_col = to_col(index_ref[1:2]).astype(jnp.int32)
    gap = (iota((SLOTS, 128), 1) + ctx * 128 - k_col) & 2047
    head = jnp.where((gap >= 1) & (gap <= 1024), acc[:, :128], acc[:, 128:]).astype(jnp.bfloat16)
    for t in range(send_ref.shape[0]):
        send_ref[t, :SLOTS] = head
        send_ref[t, SLOTS:] = tail


def value_of(count, log_total, row_log, col_log):
    value = jnp.log(jnp.maximum(count, 1.0)) + log_total - row_log - col_log - NEG_LOG
    return jnp.where(count > 0, jnp.maximum(value, 0.0), 0.0)


def core_kernel(pos_ref, slot_ref, got_ref, out_ref, stat_ref, data_ref, pick_ref):
    ctx = pos_ref[1]
    n = slot_ref.shape[1]
    words = got_ref.shape[0]
    eye = one_hot(iota((SLOTS, SLOTS), 0) == iota((SLOTS, SLOTS), 1))
    data_ref[:, 128:] = jnp.zeros((words * SLOTS, 128), jnp.bfloat16)
    total = jnp.zeros((1, 128), jnp.float32)
    for w in range(words):
        here = slice(w * SLOTS, (w + 1) * SLOTS)
        tail = got_ref[w, SLOTS:].astype(jnp.float32)
        rows = [jnp.concatenate([tail[2 * p : 2 * p + 1], tail[2 * p + 1 : 2 * p + 2]], axis=1) for p in range(4)]
        total = total + (tail[8:9] + tail[9:10] + tail[10:11])
        data_ref[here, :128] = got_ref[w, :SLOTS]
        data_ref[here, 128:144] = dot_nt(eye, stack_rows(rows, 16).astype(jnp.bfloat16)).astype(jnp.bfloat16)
    log_total = jnp.log(total)
    for t in range(n // 256):
        cut = slice(256 * t, 256 * t + 256)
        column = to_col(slot_ref[:, cut].astype(jnp.float32)).astype(jnp.int32)
        pick = dot_nn(one_hot(column == iota((256, words * SLOTS), 1)), data_ref[...])
        pick_ref[cut, :] = pick
        weight = to_row(pick[:, 128:129] + pick[:, 129:130] + pick[:, 130:131])
        on_diag = value_of(to_row(pick[:, 131:132]), log_total[:, :1], weight, weight)
        on_diag = on_diag.astype(jnp.bfloat16).astype(jnp.float32)
        stat_ref[:, cut] = stack_rows([weight, on_diag, jnp.broadcast_to(log_total[:, :1], (1, 256))], 8)
    first = pl.multiple_of(ctx * 128, 128)
    near = stat_ref[0:1, pl.ds(first, 128)]
    far = stat_ref[0:1, pl.ds(first + 1024, 128)]
    for t in range(n // 256):
        cut = slice(256 * t, 256 * t + 256)
        pick = pick_ref[cut, :]
        weight = pick[:, 128:129] + pick[:, 129:130] + pick[:, 130:131]
        gap = (iota((256, 128), 1) + ctx * 128 - iota((256, 128), 0) - 256 * t) & 2047
        other = jnp.where((gap >= 1) & (gap <= 1024), near, far)
        out_ref[cut, :] = value_of(pick[:, :128], log_total, weight, other).astype(jnp.bfloat16)


def own_kernel(pos_ref, slot_ref, stat_ref, weight_ref, *refs):
    in_refs, (out_ref,) = refs[:8], refs[8:]
    ctx = pos_ref[1]
    n = slot_ref.shape[1]
    width = in_refs[0].shape[1]
    row_log = to_col(weight_ref[0:1])
    for t in range(n // 512):
        cut = slice(512 * t, 512 * t + 512)
        acc = jnp.zeros((in_refs[0].shape[0], 512), jnp.float32)
        for r in range(8):
            source = ((ctx >> 1) - (r >> 1) & 3) * 2 + ((ctx ^ r) & 1)
            hot = one_hot(iota((width, 512), 0) + source * width == slot_ref[:, cut])
            acc += dot_nn(in_refs[r][...], hot)
        out_ref[:, cut] = value_of(acc, stat_ref[2:3, cut], row_log, stat_ref[0:1, cut]).astype(jnp.bfloat16)


def ring(x, top):
    def move(value, step):
        return lax.ppermute(value, "ctx", [(c, (c + 2 * step) % 8) for c in range(8)])

    def swap(value):
        return lax.ppermute(value, "ctx", [(c, c ^ 1) for c in range(8)])

    left, right = move(x, 1), move(x, -1)
    near = [x, left, right, move(left[:top], 1), move(right[top:], -1)]
    return near + [swap(value) for value in near]


def body(counts, row_totals, ctx_totals, samples):
    rows_dev, ctx_dev = counts.shape
    n_word = lax.axis_size("word")
    n_ctx = lax.axis_size("ctx")
    n = samples.shape[0]
    out_rows = rows_dev // n_ctx
    width = 2 * SLOTS
    pos = jnp.stack([lax.axis_index("word"), lax.axis_index("ctx")]).astype(jnp.int32)
    vmem = pl.BlockSpec(memory_space=pltpu.VMEM)
    smem = pl.BlockSpec(memory_space=pltpu.SMEM)
    half = jnp.bfloat16

    def whole(*shape):
        return pl.BlockSpec(shape, lambda g: (0,) * len(shape))

    *chunks, send, slot, index = pl.pallas_call(
        select_kernel,
        grid=(n_ctx,),
        in_specs=[smem, whole(1, n), pl.BlockSpec((out_rows, ctx_dev), lambda g: (g, 0)), whole(1, ctx_dev)],
        out_specs=[whole(out_rows, width)] * n_ctx
        + [whole(SLOTS + EXTRA, width), whole(1, n), whole(8, SLOTS)],
        out_shape=[jax.ShapeDtypeStruct((out_rows, width), half)] * n_ctx
        + [
            jax.ShapeDtypeStruct((SLOTS + EXTRA, width), half),
            jax.ShapeDtypeStruct((1, n), jnp.int32),
            jax.ShapeDtypeStruct((8, SLOTS), jnp.float32),
        ],
        scratch_shapes=[pltpu.VMEM((ctx_dev, width), half), pltpu.VMEM((rows_dev, width), half)],
        compiler_params=params(),
    )(pos, samples.reshape(1, n), counts, ctx_totals.reshape(1, ctx_dev))
    near = ring(send, TOP)
    mine = [chunks[0]]
    for r in range(1, n_ctx):
        turn = [(c, (c // 2 + r // 2) % 4 * 2 + (c ^ r) % 2) for c in range(n_ctx)]
        mine.append(lax.ppermute(chunks[r], "ctx", turn))
    send, own_weight = pl.pallas_call(
        block_kernel,
        in_specs=[smem] + [vmem] * 13,
        out_specs=[vmem, vmem],
        out_shape=[
            jax.ShapeDtypeStruct((n_word, SLOTS + EXTRA, 128), half),
            jax.ShapeDtypeStruct((8, 128), jnp.float32),
        ],
        scratch_shapes=[pltpu.VMEM((8, rows_dev), jnp.float32)],
        compiler_params=params(),
    )(pos, slot, index, row_totals.reshape(1, rows_dev), *near)
    got = lax.all_to_all(send, "word", 0, 0, tiled=True)
    part, stat = pl.pallas_call(
        core_kernel,
        in_specs=[smem, vmem, vmem],
        out_specs=[vmem, vmem],
        out_shape=[jax.ShapeDtypeStruct((n, 128), half), jax.ShapeDtypeStruct((8, n), jnp.float32)],
        scratch_shapes=[pltpu.VMEM((n_word * SLOTS, 256), half), pltpu.VMEM((n, 256), jnp.float32)],
        compiler_params=params(),
    )(pos, slot, got)
    parts = ring(part, n // 2)
    own = pl.pallas_call(
        own_kernel,
        in_specs=[smem] + [vmem] * 11,
        out_specs=vmem,
        out_shape=jax.ShapeDtypeStruct((out_rows, n), half),
        compiler_params=params(),
        cost_estimate=pl.CostEstimate(flops=4 * out_rows * n * n, bytes_accessed=2 * MEGA, transcendentals=out_rows * n),
    )(pos, slot, stat, own_weight, *mine)
    return factor(pos, parts, stat, own)


def solution(mesh):
    placed = (P("word", "ctx"), P("word"), P("ctx"), P())
    return jax.shard_map(
        body, mesh=mesh, in_specs=placed, out_specs=P(("word", "ctx"), None), check_vma=False
    )
```

```python
import math

import jax
import jax.numpy as jnp
from jax import lax
from jax.experimental import pallas as pl
from jax.experimental.pallas import tpu as pltpu
from jax.sharding import PartitionSpec as P

SAMPLES = 2048


NEG_LOG = math.log(5.0)


BLOCK = 256
SHIFT = 4.0 * math.sqrt(SAMPLES)
TOLERANCE = 1e-3
ROUNDS = (3, 2, 2, 2, 2, 2, 3, 4)


def dot_nn(left, right):
    return lax.dot_general(left, right, (((1,), (0,)), ((), ())), preferred_element_type=jnp.float32)


def dot_nt(left, right):
    return lax.dot_general(left, right, (((1,), (1,)), ((), ())), preferred_element_type=jnp.float32)


def exact_nt(left, right):
    return lax.dot_general(
        left, right, (((1,), (1,)), ((), ())), precision=lax.Precision.HIGHEST, preferred_element_type=jnp.float32
    )


def direct_factor(stat_ref, own_ref, core_ref, out_ref, tiles_ref, work_ref):
    count = core_ref.shape[0] // BLOCK
    out_rows = own_ref.shape[0]
    row_id = iota((BLOCK, 2 * BLOCK), 0)
    col_id = iota((BLOCK, 2 * BLOCK), 1)
    diag = iota((BLOCK, BLOCK), 0) == iota((BLOCK, BLOCK), 1)

    def span(i):
        return pl.ds(pl.multiple_of(i * BLOCK, BLOCK), BLOCK)

    def column(k, carry):
        block = core_ref[span(k), span(k)].astype(jnp.float32)
        block = jnp.where(diag, stat_ref[1:2, span(k)] + SHIFT, block)
        block = lax.fori_loop(
            0, k, lambda m, acc: acc - exact_nt(tiles_ref[k * count + m], tiles_ref[k * count + m]), block
        )
        work_ref[:, :BLOCK] = block
        work_ref[:, BLOCK:] = jnp.where(diag, 1.0, 0.0)

        def eliminate(j, carry):
            work = work_ref[...]
            row = jnp.sum(jnp.where(row_id == j, work, 0.0), axis=0, keepdims=True)
            col = jnp.sum(jnp.where(col_id == j, work, 0.0), axis=1, keepdims=True)
            pivot = jnp.sum(jnp.where(col_id[:1] == j, row, 0.0), axis=1, keepdims=True)
            scale = 1.0 / jnp.sqrt(pivot)
            row = row * scale
            work_ref[...] = jnp.where(row_id == j, row, jnp.where(row_id > j, work - (col * scale) * row, work))
            return carry

        lax.fori_loop(0, BLOCK, eliminate, 0)
        inv = work_ref[:, BLOCK:]

        def under(i, carry):
            tile = core_ref[span(i), span(k)].astype(jnp.float32)
            tile = lax.fori_loop(
                0, k, lambda m, acc: acc - exact_nt(tiles_ref[i * count + m], tiles_ref[k * count + m]), tile
            )
            tiles_ref[i * count + k] = exact_nt(tile, inv)
            return carry

        lax.fori_loop(k + 1, count, under, 0)
        mine = own_ref[:, span(k)].astype(jnp.float32)
        mine = lax.fori_loop(
            0, k, lambda m, acc: acc - exact_nt(out_ref[:, span(m)], tiles_ref[k * count + m]), mine
        )
        out_ref[:, span(k)] = exact_nt(mine, inv)
        return carry

    lax.fori_loop(0, count, column, 0)


def place_parts(refs, ctx, all_ref):
    for source, parts in sources(refs, ctx):
        lanes = pl.ds(pl.multiple_of(source * 128, 128), 128)
        start = 0
        for part in parts:
            all_ref[start : start + part.shape[0], lanes] = part[...]
            start += part.shape[0]


def factor_kernel(pos_ref, stat_ref, own_ref, *refs):
    part_refs, (out_ref, all_ref, core_ref, low_ref, tiles_ref, work_ref) = refs[:10], refs[10:]
    total = core_ref.shape[0]
    middle = total // 2
    half = jnp.bfloat16
    place_parts(part_refs, pos_ref[1], all_ref)
    row_id = iota((BLOCK, BLOCK), 0)
    col_id = iota((BLOCK, BLOCK), 1)
    diag = row_id == col_id
    below = row_id > col_id
    above = row_id < col_id
    eye = one_hot(diag)
    zero = jnp.zeros((BLOCK, BLOCK), half)

    def turned(tile):
        return dot_nt(eye, tile).astype(half)

    count = middle // BLOCK
    for i in range(count):
        for side in (0, middle):
            here = slice(side + i * BLOCK, side + (i + 1) * BLOCK)
            for j in range(i):
                core_ref[here, side + j * BLOCK : side + (j + 1) * BLOCK] = turned(
                    all_ref[side + j * BLOCK : side + (j + 1) * BLOCK, i * BLOCK : (i + 1) * BLOCK]
                )
            upper = jnp.where(above, all_ref[here, i * BLOCK : (i + 1) * BLOCK], zero)
            core_ref[here, here] = upper + turned(upper)
        here = slice(middle + i * BLOCK, middle + (i + 1) * BLOCK)
        for j in range(count):
            cols = slice(j * BLOCK, (j + 1) * BLOCK)
            if i > j:
                tile = all_ref[here, cols]
            else:
                tile = turned(all_ref[cols, i * BLOCK : (i + 1) * BLOCK])
            if i == j:
                tile = jnp.where(above, tile, all_ref[here, cols])
            core_ref[here, cols] = tile

    weight = jnp.where(below, 1.0, jnp.where(diag, 0.5, 0.0))
    worst = jnp.zeros((1, 1), jnp.float32)
    for k in range(total // BLOCK):
        lo, hi = k * BLOCK, (k + 1) * BLOCK
        block = core_ref[lo:hi, lo:hi].astype(jnp.float32)
        block = jnp.where(diag, stat_ref[1:2, lo:hi] + SHIFT, block)
        if k:
            pivot = low_ref[lo:hi, :lo]
            block = block - dot_nt(pivot, pivot)
        on_diag = jnp.where(diag, block, 0.0)
        scale_col = lax.rsqrt(jnp.sum(on_diag, axis=1, keepdims=True))
        scale_row = lax.rsqrt(jnp.sum(on_diag, axis=0, keepdims=True))
        off = jnp.where(diag, 0.0, block * scale_col * scale_row)
        off_half = off.astype(half)
        inv = jnp.where(below, -off, 0.0)
        for _ in range(ROUNDS[k]):
            inv_half = inv.astype(half)
            inner = off + dot_nn(inv_half, off_half)
            resid = inner + dot_nt((inner + inv).astype(half), inv_half)
            step = inv + resid * weight
            inv = inv - step - dot_nn(step.astype(half), inv_half)
        worst = jnp.maximum(worst, jnp.sum(step * step, keepdims=True))
        inv_half = inv.astype(half)
        if hi < total:
            under = core_ref[hi:, lo:hi].astype(jnp.float32)
            if k:
                under = under - dot_nt(low_ref[hi:total, :lo], pivot)
            under = under * scale_row
            low_ref[hi:total, lo:hi] = (under + dot_nt(under.astype(half), inv_half)).astype(half)
        mine = own_ref[:, lo:hi].astype(jnp.float32)
        if k:
            mine = mine - dot_nt(low_ref[total:, :lo], pivot)
        mine = mine * scale_row
        mine = mine + dot_nt(mine.astype(half), inv_half)
        out_ref[:, lo:hi] = mine
        low_ref[total:, lo:hi] = mine.astype(half)

    @pl.when(jnp.logical_not(worst[0, 0] < TOLERANCE))
    def _():
        direct_factor(stat_ref, own_ref, core_ref, out_ref, tiles_ref, work_ref)


def factor(pos, parts, stat, own):
    out_rows, total = own.shape
    count = total // BLOCK
    vmem = pl.BlockSpec(memory_space=pltpu.VMEM)
    smem = pl.BlockSpec(memory_space=pltpu.SMEM)
    return pl.pallas_call(
        factor_kernel,
        out_shape=jax.ShapeDtypeStruct((out_rows, total), jnp.float32),
        in_specs=[smem] + [vmem] * 12,
        out_specs=vmem,
        scratch_shapes=[
            pltpu.VMEM((total, total // 2), jnp.bfloat16),
            pltpu.VMEM((total, total), jnp.bfloat16),
            pltpu.VMEM((total + out_rows, total), jnp.bfloat16),
            pltpu.VMEM((count * count, BLOCK, BLOCK), jnp.float32),
            pltpu.VMEM((BLOCK, 2 * BLOCK), jnp.float32),
        ],
        compiler_params=params(60),
    )(pos, stat, own, *parts)


SLOTS = 256
EXTRA = 16
MEGA = 1024 * 1024


def params(limit=48):
    return pltpu.CompilerParams(vmem_limit_bytes=limit * MEGA)


def iota(shape, dim):
    return lax.broadcasted_iota(jnp.int32, shape, dim)


def to_col(row):
    n = row.shape[1]
    square = iota((n, n), 0) == iota((n, n), 1)
    return jnp.sum(jnp.where(square, jnp.broadcast_to(row, (n, n)), 0.0), axis=1, keepdims=True)


def to_row(col):
    n = col.shape[0]
    square = iota((n, n), 0) == iota((n, n), 1)
    return jnp.sum(jnp.where(square, jnp.broadcast_to(col, (n, n)), 0.0), axis=0, keepdims=True)


def stack_rows(rows, height):
    width = rows[0].shape[1]
    index = iota((height, width), 0)
    out = jnp.zeros((height, width), jnp.float32)
    for r, row in enumerate(rows):
        out = jnp.where(index == r, jnp.broadcast_to(row, (height, width)), out)
    return out


def one_hot(mask):
    return jnp.where(mask, 1.0, 0.0).astype(jnp.bfloat16)


def pieces(value):
    high = value.astype(jnp.bfloat16).astype(jnp.float32)
    rest = value - high
    middle = rest.astype(jnp.bfloat16).astype(jnp.float32)
    return [high, middle, rest - middle]


def select_kernel(pos_ref, samples_ref, counts_ref, row_ref, ctx_ref, *refs):
    chunk_refs, (send_ref, slot_ref, index_ref, hot_ref, picked_ref) = refs[:4], refs[4:]
    g = pl.program_id(0)
    word, ctx = pos_ref[0], pos_ref[1]
    n = samples_ref.shape[1]
    rows = counts_ref.shape[0]
    width = hot_ref.shape[1]
    share = chunk_refs[0].shape[0] // 2

    @pl.when(g == 0)
    def _():
        sample = samples_ref[...]
        block = sample >> 10
        member = jnp.where(iota((16, n), 0) == block, 1.0, 0.0)
        before = one_hot(iota((256, 256), 0) < iota((256, 256), 1))
        count = jnp.zeros((16, 1), jnp.float32)
        k = iota((1, n), 1)
        local = sample & 2047
        vals = stack_rows(
            [v.astype(jnp.float32) for v in (local >> 8, local & 255, local * 0 + 1, k >> 8, k & 255, (local & 1023) >> 8)],
            8,
        ).astype(jnp.bfloat16)
        by_ctx = jnp.zeros((8, width), jnp.float32)
        by_word = jnp.zeros((8, SLOTS), jnp.float32)
        for t in range(n // 256):
            cut = slice(256 * t, 256 * t + 256)
            mine = member[:, cut]
            rank = dot_nn(mine.astype(jnp.bfloat16), before) + count
            count = count + jnp.sum(mine, axis=1, keepdims=True)
            slot = block[:, cut].astype(jnp.float32) * SLOTS + jnp.sum(mine * rank, axis=0, keepdims=True)
            slot_ref[:, cut] = slot.astype(jnp.int32)
            column = to_col(slot).astype(jnp.int32)
            by_ctx += dot_nn(vals[:, cut], one_hot(column - ctx * width == iota((256, width), 1)))
            by_word += dot_nn(vals[:, cut], one_hot(column - word * SLOTS == iota((256, SLOTS), 1)))
        col = jnp.where(by_ctx[2:3] > 0, by_ctx[0:1] * 256 + by_ctx[1:2], -1.0).astype(jnp.int32)
        for t in range(hot_ref.shape[0] // 256):
            hot_ref[256 * t : 256 * t + 256] = one_hot(iota((256, width), 0) + 256 * t == col)
        row = jnp.where(by_word[2:3] > 0, by_word[5:6] * 256 + by_word[1:2], -1.0)
        index_ref[...] = stack_rows([row, by_word[3:4] * 256 + by_word[4:5]], 8)

    chunk = dot_nn(counts_ref[...].astype(jnp.float32).astype(jnp.bfloat16), hot_ref[...]).astype(jnp.bfloat16)
    picked_ref[pl.ds(pl.multiple_of(g * rows, rows), rows), :] = chunk
    for r in range(4):

        @pl.when((g - (ctx >> 1) & 3) == r)
        def _(r=r):
            odd = (ctx & 1) == 1
            chunk_refs[r][:share] = jnp.where(odd, chunk[share:], chunk[:share])
            chunk_refs[r][share:] = jnp.where(odd, chunk[:share], chunk[share:])

    @pl.when(g == pl.num_programs(0) - 1)
    def _():
        total_rows = picked_ref.shape[0]
        row_hot = one_hot(to_col(index_ref[0:1]).astype(jnp.int32) == iota((SLOTS, total_rows), 1))
        picked = dot_nn(row_hot, picked_ref[...])
        tile = jnp.where((word & 1) == 1, picked[:, SLOTS:], picked[:, :SLOTS])
        square = iota((SLOTS, SLOTS), 0) == iota((SLOTS, SLOTS), 1)
        own_diag = jnp.sum(jnp.where(square, tile, 0.0), axis=0, keepdims=True)
        here = ctx_ref[:, pl.ds(pl.multiple_of((word & 1) * total_rows, total_rows), total_rows)]
        weight = 0.5 * (jnp.log(row_ref[...].astype(jnp.float32)) + jnp.log(here.astype(jnp.float32)))
        weight_parts = pieces(weight)
        slot_weight = dot_nt(stack_rows(weight_parts, 16).astype(jnp.bfloat16), row_hot)
        parts = []
        for p in range(3):
            parts += [slot_weight[p : p + 1, :128], slot_weight[p : p + 1, 128:]]
        parts += [own_diag[:, :128], own_diag[:, 128:]]
        holder = ctx == word >> 1
        full = dot_nn(
            picked.astype(jnp.bfloat16), one_hot(iota((width, n), 0) + ctx * width == slot_ref[...])
        )
        k_col = to_col(index_ref[1:2]).astype(jnp.int32)
        gap = (iota((SLOTS, n // 2), 1) - k_col) & (n - 1)
        head = jnp.where((gap >= 1) & (gap <= n // 2), full[:, : n // 2], full[:, n // 2 :]).astype(jnp.bfloat16)
        for c in range(8):
            lanes = slice(128 * c, 128 * c + 128)
            tail = stack_rows(parts + [p[:, lanes] for p in weight_parts], EXTRA)
            send_ref[c, :SLOTS] = head[:, lanes]
            send_ref[c, SLOTS:] = jnp.where(holder, tail, 0.0).astype(jnp.bfloat16)


def sources(refs, ctx):
    z, core = ctx >> 1, ctx & 1
    out = []
    for half in (0, 1):
        own, left, right, top, bottom = refs[5 * half : 5 * half + 5]
        for step, parts in ((0, (own,)), (3, (left,)), (1, (right,)), (2, (top, bottom))):
            out.append((((z + step) & 3) * 2 + (core ^ half), parts))
    return out


def block_kernel(totals_ref, got_ref, send_ref, own_ref):
    got = got_ref[0].astype(jnp.float32)
    for c in range(1, got_ref.shape[0]):
        got = got + got_ref[c].astype(jnp.float32)
    tail = got[SLOTS:]
    own_ref[...] = jnp.broadcast_to(tail[8:9] + tail[9:10] + tail[10:11], own_ref.shape)
    total = pieces(jnp.sum(totals_ref[...].astype(jnp.float32), axis=1, keepdims=True))
    row = iota(tail.shape, 0)
    for p in range(3):
        tail = jnp.where(row == 8 + p, jnp.broadcast_to(total[p], tail.shape), tail)
    send_ref[:SLOTS] = got[:SLOTS].astype(jnp.bfloat16)
    send_ref[SLOTS:] = tail.astype(jnp.bfloat16)


def value_of(count, log_total, row_log, col_log):
    value = jnp.log(jnp.maximum(count, 1.0)) + log_total - row_log - col_log - NEG_LOG
    return jnp.where(count > 0, jnp.maximum(value, 0.0), 0.0)


def word_sources(refs, word):
    y, x = word >> 2, word & 3
    own, left, right, top, bottom = refs
    for step, parts in ((0, (own,)), (3, (left,)), (1, (right,)), (2, (top, bottom))):
        for i, across in enumerate((0, 3, 1, 2)):
            part, place = (parts[0], i) if len(parts) == 1 else (parts[i // 2], i % 2)
            yield ((y + step) & 3) * 4 + ((x + across) & 3), part, place * (SLOTS + EXTRA)


def core_kernel(pos_ref, slot_ref, *refs):
    in_refs, (out_ref, stat_ref, data_ref, pick_ref) = refs[:5], refs[5:]
    ctx = pos_ref[1]
    n = slot_ref.shape[1]
    words = data_ref.shape[0] // SLOTS
    eye = one_hot(iota((SLOTS, SLOTS), 0) == iota((SLOTS, SLOTS), 1))
    data_ref[:, 128:] = jnp.zeros((words * SLOTS, 128), jnp.bfloat16)
    total = jnp.zeros((1, 128), jnp.float32)
    for source, part, start in word_sources(in_refs, pos_ref[0]):
        here = pl.ds(pl.multiple_of(source * SLOTS, SLOTS), SLOTS)
        tail = part[start + SLOTS : start + SLOTS + EXTRA].astype(jnp.float32)
        rows = [jnp.concatenate([tail[2 * p : 2 * p + 1], tail[2 * p + 1 : 2 * p + 2]], axis=1) for p in range(4)]
        total = total + (tail[8:9] + tail[9:10] + tail[10:11])
        data_ref[here, :128] = part[start : start + SLOTS]
        data_ref[here, 128:144] = dot_nt(eye, stack_rows(rows, 16).astype(jnp.bfloat16)).astype(jnp.bfloat16)
    log_total = jnp.log(total)
    for t in range(n // 256):
        cut = slice(256 * t, 256 * t + 256)
        column = to_col(slot_ref[:, cut].astype(jnp.float32)).astype(jnp.int32)
        pick = dot_nn(one_hot(column == iota((256, words * SLOTS), 1)), data_ref[...])
        pick_ref[cut, :] = pick
        weight = to_row(pick[:, 128:129] + pick[:, 129:130] + pick[:, 130:131])
        on_diag = value_of(to_row(pick[:, 131:132]), log_total[:, :1], weight, weight)
        on_diag = on_diag.astype(jnp.bfloat16).astype(jnp.float32)
        stat_ref[:, cut] = stack_rows([weight, on_diag, jnp.broadcast_to(log_total[:, :1], (1, 256))], 8)
    first = pl.multiple_of(ctx * 128, 128)
    near = stat_ref[0:1, pl.ds(first, 128)]
    far = stat_ref[0:1, pl.ds(first + 1024, 128)]
    for t in range(n // 256):
        cut = slice(256 * t, 256 * t + 256)
        pick = pick_ref[cut, :]
        weight = pick[:, 128:129] + pick[:, 129:130] + pick[:, 130:131]
        gap = (iota((256, 128), 1) + ctx * 128 - iota((256, 128), 0) - 256 * t) & 2047
        other = jnp.where((gap >= 1) & (gap <= 1024), near, far)
        out_ref[cut, :] = value_of(pick[:, :128], log_total, weight, other).astype(jnp.bfloat16)


def own_kernel(pos_ref, slot_ref, stat_ref, weight_ref, *refs):
    in_refs, swapped_ref, out_ref = refs[:4], refs[4], refs[5]
    ctx = pos_ref[1]
    n = slot_ref.shape[1]
    out_rows, width = out_ref.shape[0], in_refs[0].shape[1]
    row_log = to_col(weight_ref[0:1])
    for t in range(n // 512):
        cut = slice(512 * t, 512 * t + 512)
        acc = jnp.zeros((out_rows, 512), jnp.float32)
        for r in range(8):
            source = ((ctx >> 1) - (r >> 1) & 3) * 2 + ((ctx ^ r) & 1)
            hot = one_hot(iota((width, 512), 0) + source * width == slot_ref[:, cut])
            step = r // 2
            part = swapped_ref[step * out_rows : (step + 1) * out_rows] if r % 2 else in_refs[step][:out_rows]
            acc += dot_nn(part, hot)
        out_ref[:, cut] = value_of(acc, stat_ref[2:3, cut], row_log, stat_ref[0:1, cut]).astype(jnp.bfloat16)


def move(value, step):
    return lax.ppermute(value, "ctx", [(c, (c + 2 * step) % 8) for c in range(8)])


def swap(value):
    return lax.ppermute(value, "ctx", [(c, c ^ 1) for c in range(8)])


def across(value, step):
    return lax.ppermute(value, "word", [(w, w // 4 * 4 + (w + step) % 4) for w in range(16)])


def along(value, step):
    return lax.ppermute(value, "word", [(w, (w + 4 * step) % 16) for w in range(16)])


def body(counts, row_totals, ctx_totals, samples):
    rows_dev, ctx_dev = counts.shape
    n_word = lax.axis_size("word")
    n_ctx = lax.axis_size("ctx")
    n = samples.shape[0]
    out_rows = rows_dev // n_ctx
    width = 2 * SLOTS
    pos = jnp.stack([lax.axis_index("word"), lax.axis_index("ctx")]).astype(jnp.int32)
    vmem = pl.BlockSpec(memory_space=pltpu.VMEM)
    smem = pl.BlockSpec(memory_space=pltpu.SMEM)
    half = jnp.bfloat16

    def whole(*shape):
        return pl.BlockSpec(shape, lambda g: (0,) * len(shape))

    *chunks, send, slot = pl.pallas_call(
        select_kernel,
        grid=(n_ctx // 2,),
        in_specs=[
            smem,
            whole(1, n),
            pl.BlockSpec((2 * out_rows, ctx_dev), lambda g: (g, 0)),
            whole(1, rows_dev),
            whole(1, ctx_dev),
        ],
        out_specs=[whole(2 * out_rows, width)] * 4 + [whole(n_ctx, SLOTS + EXTRA, 128), whole(1, n)],
        out_shape=[jax.ShapeDtypeStruct((2 * out_rows, width), half)] * 4
        + [
            jax.ShapeDtypeStruct((n_ctx, SLOTS + EXTRA, 128), half),
            jax.ShapeDtypeStruct((1, n), jnp.int32),
        ],
        scratch_shapes=[
            pltpu.VMEM((8, SLOTS), jnp.float32),
            pltpu.VMEM((ctx_dev, width), half),
            pltpu.VMEM((rows_dev, width), half),
        ],
        compiler_params=params(60),
    )(pos, samples.reshape(1, n), counts, row_totals.reshape(1, rows_dev), ctx_totals.reshape(1, ctx_dev))
    got = lax.all_to_all(send, "ctx", 0, 0, tiled=True)
    send, own_weight = pl.pallas_call(
        block_kernel,
        in_specs=[vmem] * 2,
        out_specs=[vmem, vmem],
        out_shape=[
            jax.ShapeDtypeStruct((SLOTS + EXTRA, 128), half),
            jax.ShapeDtypeStruct((8, 128), jnp.float32),
        ],
        compiler_params=params(),
    )(row_totals.reshape(1, rows_dev), got)
    line = jnp.concatenate([send] + [across(send, step) for step in (1, -1, 2)], axis=0)
    left, right = along(line, 1), along(line, -1)
    middle = line.shape[0] // 2
    chunks, line = lax.optimization_barrier((chunks, line))
    mine = [chunks[0]] + [move(chunks[step], step) for step in (1, 2, 3)]
    lines = [line, left, right, along(left[:middle], 1), along(right[middle:], -1)]
    lines, mine = lax.optimization_barrier((lines, mine))
    part, stat = pl.pallas_call(
        core_kernel,
        in_specs=[smem] + [vmem] * 6,
        out_specs=[vmem, vmem],
        out_shape=[jax.ShapeDtypeStruct((n, 128), half), jax.ShapeDtypeStruct((8, n), jnp.float32)],
        scratch_shapes=[pltpu.VMEM((n_word * SLOTS, 256), half), pltpu.VMEM((n, 256), jnp.float32)],
        compiler_params=params(),
    )(pos, slot, *lines)
    left, right = move(part, 1), move(part, -1)
    mine, part = lax.optimization_barrier((mine, part))
    swapped = swap(jnp.concatenate([value[out_rows:] for value in mine], axis=0))
    own = pl.pallas_call(
        own_kernel,
        in_specs=[smem] + [vmem] * 8,
        out_specs=vmem,
        out_shape=jax.ShapeDtypeStruct((out_rows, n), half),
        compiler_params=params(),
        cost_estimate=pl.CostEstimate(flops=4 * out_rows * n * n, bytes_accessed=2 * MEGA, transcendentals=out_rows * n),
    )(pos, slot, stat, own_weight, *mine, swapped)
    left, right, own = lax.optimization_barrier((left, right, own))
    parts = [part, left, right, move(left[: n // 2], 1), move(right[n // 2 :], -1)]
    parts = parts + [swap(value) for value in parts]
    return factor(pos, parts, stat, own)


def solution(mesh):
    placed = (P("word", "ctx"), P("word"), P("ctx"), P())
    return jax.shard_map(
        body, mesh=mesh, in_specs=placed, out_specs=P(("word", "ctx"), None), check_vma=False
    )
```

```python
import math

import jax
import jax.numpy as jnp
from jax import lax
from jax.experimental import pallas as pl
from jax.experimental.pallas import tpu as pltpu
from jax.sharding import PartitionSpec as P

SAMPLES = 2048


NEG_LOG = math.log(5.0)


BLOCK = 256
SHIFT = 4.0 * math.sqrt(SAMPLES)
TOLERANCE = 1e-3
ROUNDS = (3, 2, 2, 2, 2, 2, 2, 3)


def dot_nn(left, right):
    return lax.dot_general(left, right, (((1,), (0,)), ((), ())), preferred_element_type=jnp.float32)


def dot_nt(left, right):
    return lax.dot_general(left, right, (((1,), (1,)), ((), ())), preferred_element_type=jnp.float32)


def exact_nt(left, right):
    return lax.dot_general(
        left, right, (((1,), (1,)), ((), ())), precision=lax.Precision.HIGHEST, preferred_element_type=jnp.float32
    )


def direct_factor(stat_ref, own_ref, core_ref, out_ref, tiles_ref, work_ref):
    count = core_ref.shape[0] // BLOCK
    out_rows = own_ref.shape[0]
    row_id = iota((BLOCK, 2 * BLOCK), 0)
    col_id = iota((BLOCK, 2 * BLOCK), 1)
    diag = iota((BLOCK, BLOCK), 0) == iota((BLOCK, BLOCK), 1)

    def span(i):
        return pl.ds(pl.multiple_of(i * BLOCK, BLOCK), BLOCK)

    def place(i, k):
        return i * (i - 1) // 2 + k

    def column(k, carry):
        block = core_ref[span(k), span(k)].astype(jnp.float32)
        block = jnp.where(diag, stat_ref[1:2, span(k)] + SHIFT, block)
        block = lax.fori_loop(
            0, k, lambda m, acc: acc - exact_nt(tiles_ref[place(k, m)], tiles_ref[place(k, m)]), block
        )
        work_ref[:, :BLOCK] = block
        work_ref[:, BLOCK:] = jnp.where(diag, 1.0, 0.0)

        def eliminate(j, carry):
            work = work_ref[...]
            row = jnp.sum(jnp.where(row_id == j, work, 0.0), axis=0, keepdims=True)
            col = jnp.sum(jnp.where(col_id == j, work, 0.0), axis=1, keepdims=True)
            pivot = jnp.sum(jnp.where(col_id[:1] == j, row, 0.0), axis=1, keepdims=True)
            scale = 1.0 / jnp.sqrt(pivot)
            row = row * scale
            work_ref[...] = jnp.where(row_id == j, row, jnp.where(row_id > j, work - (col * scale) * row, work))
            return carry

        lax.fori_loop(0, BLOCK, eliminate, 0)
        inv = work_ref[:, BLOCK:]

        def under(i, carry):
            tile = core_ref[span(i), span(k)].astype(jnp.float32)
            tile = lax.fori_loop(
                0, k, lambda m, acc: acc - exact_nt(tiles_ref[place(i, m)], tiles_ref[place(k, m)]), tile
            )
            tiles_ref[place(i, k)] = exact_nt(tile, inv)
            return carry

        lax.fori_loop(k + 1, count, under, 0)
        mine = own_ref[:, span(k)].astype(jnp.float32)
        mine = lax.fori_loop(
            0, k, lambda m, acc: acc - exact_nt(out_ref[:, span(m)], tiles_ref[place(k, m)]), mine
        )
        out_ref[:, span(k)] = exact_nt(mine, inv)
        return carry

    lax.fori_loop(0, count, column, 0)


def place_parts(refs, ctx, all_ref):
    for source, parts in sources(refs, ctx):
        lanes = pl.ds(pl.multiple_of(source * 128, 128), 128)
        start = 0
        for part in parts:
            all_ref[start : start + part.shape[0], lanes] = part[...]
            start += part.shape[0]


def factor_kernel(pos_ref, stat_ref, own_ref, *refs):
    part_refs, (out_ref, all_ref, core_ref, low_ref, tiles_ref, work_ref) = refs[:10], refs[10:]
    total = core_ref.shape[0]
    middle = total // 2
    half = jnp.bfloat16
    place_parts(part_refs, pos_ref[1], all_ref)
    row_id = iota((BLOCK, BLOCK), 0)
    col_id = iota((BLOCK, BLOCK), 1)
    diag = row_id == col_id
    below = row_id > col_id
    above = row_id < col_id
    eye = one_hot(diag)
    zero = jnp.zeros((BLOCK, BLOCK), half)

    def turned(tile):
        return dot_nt(eye, tile).astype(half)

    count = middle // BLOCK
    for i in range(count):
        for side in (0, middle):
            here = slice(side + i * BLOCK, side + (i + 1) * BLOCK)
            for j in range(i):
                core_ref[here, side + j * BLOCK : side + (j + 1) * BLOCK] = turned(
                    all_ref[side + j * BLOCK : side + (j + 1) * BLOCK, i * BLOCK : (i + 1) * BLOCK]
                )
            upper = jnp.where(above, all_ref[here, i * BLOCK : (i + 1) * BLOCK], zero)
            core_ref[here, here] = upper + turned(upper)
        here = slice(middle + i * BLOCK, middle + (i + 1) * BLOCK)
        for j in range(count):
            cols = slice(j * BLOCK, (j + 1) * BLOCK)
            if i > j:
                tile = all_ref[here, cols]
            else:
                tile = turned(all_ref[cols, i * BLOCK : (i + 1) * BLOCK])
            if i == j:
                tile = jnp.where(above, tile, all_ref[here, cols])
            core_ref[here, cols] = tile

    weight = jnp.where(below, 1.0, jnp.where(diag, 0.5, 0.0))
    worst = jnp.zeros((1, 1), jnp.float32)
    for k in range(total // BLOCK):
        lo, hi = k * BLOCK, (k + 1) * BLOCK
        block = core_ref[lo:hi, lo:hi].astype(jnp.float32)
        block = jnp.where(diag, stat_ref[1:2, lo:hi] + SHIFT, block)
        if k:
            pivot = low_ref[lo:hi, :lo]
            block = block - dot_nt(pivot, pivot)
        on_diag = jnp.where(diag, block, 0.0)
        scale_col = lax.rsqrt(jnp.sum(on_diag, axis=1, keepdims=True))
        scale_row = lax.rsqrt(jnp.sum(on_diag, axis=0, keepdims=True))
        off = jnp.where(diag, 0.0, block * scale_col * scale_row)
        step = off * weight
        inv = -step
        for _ in range(ROUNDS[k]):
            step_half = step.astype(half)
            inner = dot_nn(step_half, off.astype(half))
            off = dot_nt((inner + step - off).astype(half), step_half) - inner
            step = off * weight
            inv = inv - step - dot_nn(step.astype(half), inv.astype(half))
        worst = jnp.maximum(worst, jnp.sum(step * step, keepdims=True))
        inv_half = inv.astype(half)
        if hi < total:
            under = core_ref[hi:, lo:hi].astype(jnp.float32)
            if k:
                under = under - dot_nt(low_ref[hi:total, :lo], pivot)
            under = under * scale_row
            low_ref[hi:total, lo:hi] = (under + dot_nt(under.astype(half), inv_half)).astype(half)
        mine = own_ref[:, lo:hi].astype(jnp.float32)
        if k:
            mine = mine - dot_nt(low_ref[total:, :lo], pivot)
        mine = mine * scale_row
        mine = mine + dot_nt(mine.astype(half), inv_half)
        out_ref[:, lo:hi] = mine
        low_ref[total:, lo:hi] = mine.astype(half)

    @pl.when(jnp.logical_not(worst[0, 0] < TOLERANCE))
    def _():
        direct_factor(stat_ref, own_ref, core_ref, out_ref, tiles_ref, work_ref)


def factor(pos, parts, stat, own):
    out_rows, total = own.shape
    count = total // BLOCK
    vmem = pl.BlockSpec(memory_space=pltpu.VMEM)
    smem = pl.BlockSpec(memory_space=pltpu.SMEM)
    return pl.pallas_call(
        factor_kernel,
        out_shape=jax.ShapeDtypeStruct((out_rows, total), jnp.float32),
        in_specs=[smem] + [vmem] * 12,
        out_specs=vmem,
        scratch_shapes=[
            pltpu.VMEM((total, total // 2), jnp.bfloat16),
            pltpu.VMEM((total, total), jnp.bfloat16),
            pltpu.VMEM((total + out_rows, total), jnp.bfloat16),
            pltpu.VMEM((count * (count - 1) // 2, BLOCK, BLOCK), jnp.float32),
            pltpu.VMEM((BLOCK, 2 * BLOCK), jnp.float32),
        ],
        compiler_params=params(40),
    )(pos, stat, own, *parts)


SLOTS = 256
EXTRA = 16
MEGA = 1024 * 1024


def params(limit=48):
    return pltpu.CompilerParams(vmem_limit_bytes=limit * MEGA)


def iota(shape, dim):
    return lax.broadcasted_iota(jnp.int32, shape, dim)


def to_col(row):
    n = row.shape[1]
    square = iota((n, n), 0) == iota((n, n), 1)
    return jnp.sum(jnp.where(square, jnp.broadcast_to(row, (n, n)), 0.0), axis=1, keepdims=True)


def to_row(col):
    n = col.shape[0]
    square = iota((n, n), 0) == iota((n, n), 1)
    return jnp.sum(jnp.where(square, jnp.broadcast_to(col, (n, n)), 0.0), axis=0, keepdims=True)


def stack_rows(rows, height):
    width = rows[0].shape[1]
    index = iota((height, width), 0)
    out = jnp.zeros((height, width), jnp.float32)
    for r, row in enumerate(rows):
        out = jnp.where(index == r, jnp.broadcast_to(row, (height, width)), out)
    return out


def one_hot(mask):
    return jnp.where(mask, 1.0, 0.0).astype(jnp.bfloat16)


def pieces(value):
    high = value.astype(jnp.bfloat16).astype(jnp.float32)
    rest = value - high
    middle = rest.astype(jnp.bfloat16).astype(jnp.float32)
    return [high, middle, rest - middle]


def select_kernel(pos_ref, samples_ref, counts_ref, row_ref, ctx_ref, *refs):
    chunk_refs, (send_ref, slot_ref, index_ref, hot_ref, picked_ref) = refs[:4], refs[4:]
    g = pl.program_id(0)
    word, ctx = pos_ref[0], pos_ref[1]
    n = samples_ref.shape[1]
    rows = counts_ref.shape[0]
    width = hot_ref.shape[1]
    share = chunk_refs[0].shape[0] // 2

    @pl.when(g == 0)
    def _():
        sample = samples_ref[...]
        block = sample >> 10
        member = jnp.where(iota((16, n), 0) == block, 1.0, 0.0)
        before = one_hot(iota((256, 256), 0) < iota((256, 256), 1))
        count = jnp.zeros((16, 1), jnp.float32)
        k = iota((1, n), 1)
        local = sample & 2047
        vals = stack_rows(
            [v.astype(jnp.float32) for v in (local >> 8, local & 255, local * 0 + 1, k >> 8, k & 255, (local & 1023) >> 8)],
            8,
        ).astype(jnp.bfloat16)
        by_ctx = jnp.zeros((8, width), jnp.float32)
        by_word = jnp.zeros((8, SLOTS), jnp.float32)
        for t in range(n // 256):
            cut = slice(256 * t, 256 * t + 256)
            mine = member[:, cut]
            rank = dot_nn(mine.astype(jnp.bfloat16), before) + count
            count = count + jnp.sum(mine, axis=1, keepdims=True)
            slot = block[:, cut].astype(jnp.float32) * SLOTS + jnp.sum(mine * rank, axis=0, keepdims=True)
            slot_ref[:, cut] = slot.astype(jnp.int32)
            column = to_col(slot).astype(jnp.int32)
            by_ctx += dot_nn(vals[:, cut], one_hot(column - ctx * width == iota((256, width), 1)))
            by_word += dot_nn(vals[:, cut], one_hot(column - word * SLOTS == iota((256, SLOTS), 1)))
        col = jnp.where(by_ctx[2:3] > 0, by_ctx[0:1] * 256 + by_ctx[1:2], -1.0).astype(jnp.int32)
        for t in range(hot_ref.shape[0] // 256):
            hot_ref[256 * t : 256 * t + 256] = one_hot(iota((256, width), 0) + 256 * t == col)
        row = jnp.where(by_word[2:3] > 0, by_word[5:6] * 256 + by_word[1:2], -1.0)
        index_ref[...] = stack_rows([row, by_word[3:4] * 256 + by_word[4:5]], 8)

    chunk = dot_nn(counts_ref[...].astype(jnp.float32).astype(jnp.bfloat16), hot_ref[...]).astype(jnp.bfloat16)
    picked_ref[pl.ds(pl.multiple_of(g * rows, rows), rows), :] = chunk
    for r in range(4):

        @pl.when((g - (ctx >> 1) & 3) == r)
        def _(r=r):
            odd = (ctx & 1) == 1
            chunk_refs[r][:share] = jnp.where(odd, chunk[share:], chunk[:share])
            chunk_refs[r][share:] = jnp.where(odd, chunk[:share], chunk[share:])

    @pl.when(g == pl.num_programs(0) - 1)
    def _():
        total_rows = picked_ref.shape[0]
        row_hot = one_hot(to_col(index_ref[0:1]).astype(jnp.int32) == iota((SLOTS, total_rows), 1))
        picked = dot_nn(row_hot, picked_ref[...])
        tile = jnp.where((word & 1) == 1, picked[:, SLOTS:], picked[:, :SLOTS])
        square = iota((SLOTS, SLOTS), 0) == iota((SLOTS, SLOTS), 1)
        own_diag = jnp.sum(jnp.where(square, tile, 0.0), axis=0, keepdims=True)
        here = ctx_ref[:, pl.ds(pl.multiple_of((word & 1) * total_rows, total_rows), total_rows)]
        weight = 0.5 * (jnp.log(row_ref[...].astype(jnp.float32)) + jnp.log(here.astype(jnp.float32)))
        weight_parts = pieces(weight)
        slot_weight = dot_nt(stack_rows(weight_parts, 16).astype(jnp.bfloat16), row_hot)
        parts = []
        for p in range(3):
            parts += [slot_weight[p : p + 1, :128], slot_weight[p : p + 1, 128:]]
        parts += [own_diag[:, :128], own_diag[:, 128:]]
        holder = ctx == word >> 1
        full = dot_nn(
            picked.astype(jnp.bfloat16), one_hot(iota((width, n), 0) + ctx * width == slot_ref[...])
        )
        k_col = to_col(index_ref[1:2]).astype(jnp.int32)
        gap = (iota((SLOTS, n // 2), 1) - k_col) & (n - 1)
        head = jnp.where((gap >= 1) & (gap <= n // 2), full[:, : n // 2], full[:, n // 2 :]).astype(jnp.bfloat16)
        for c in range(8):
            lanes = slice(128 * c, 128 * c + 128)
            tail = stack_rows(parts + [p[:, lanes] for p in weight_parts], EXTRA)
            send_ref[c, :SLOTS] = head[:, lanes]
            send_ref[c, SLOTS:] = jnp.where(holder, tail, 0.0).astype(jnp.bfloat16)


def sources(refs, ctx):
    z, core = ctx >> 1, ctx & 1
    out = []
    for half in (0, 1):
        own, left, right, top, bottom = refs[5 * half : 5 * half + 5]
        for step, parts in ((0, (own,)), (3, (left,)), (1, (right,)), (2, (top, bottom))):
            out.append((((z + step) & 3) * 2 + (core ^ half), parts))
    return out


def block_kernel(totals_ref, got_ref, send_ref, own_ref):
    got = got_ref[0].astype(jnp.float32)
    for c in range(1, got_ref.shape[0]):
        got = got + got_ref[c].astype(jnp.float32)
    tail = got[SLOTS:]
    own_ref[...] = jnp.broadcast_to(tail[8:9] + tail[9:10] + tail[10:11], own_ref.shape)
    total = pieces(jnp.sum(totals_ref[...].astype(jnp.float32), axis=1, keepdims=True))
    row = iota(tail.shape, 0)
    for p in range(3):
        tail = jnp.where(row == 8 + p, jnp.broadcast_to(total[p], tail.shape), tail)
    send_ref[:SLOTS] = got[:SLOTS].astype(jnp.bfloat16)
    send_ref[SLOTS:] = tail.astype(jnp.bfloat16)


def value_of(count, log_total, row_log, col_log):
    value = jnp.log(jnp.maximum(count, 1.0)) + log_total - row_log - col_log - NEG_LOG
    return jnp.where(count > 0, jnp.maximum(value, 0.0), 0.0)


def word_sources(refs, word):
    y, x = word >> 2, word & 3
    own, left, right, top, bottom = refs
    for step, parts in ((0, (own,)), (3, (left,)), (1, (right,)), (2, (top, bottom))):
        for i, across in enumerate((0, 3, 1, 2)):
            part, place = (parts[0], i) if len(parts) == 1 else (parts[i // 2], i % 2)
            yield ((y + step) & 3) * 4 + ((x + across) & 3), part, place * (SLOTS + EXTRA)


def core_kernel(pos_ref, slot_ref, *refs):
    in_refs, (out_ref, stat_ref, data_ref, pick_ref) = refs[:5], refs[5:]
    ctx = pos_ref[1]
    n = slot_ref.shape[1]
    words = data_ref.shape[0] // SLOTS
    eye = one_hot(iota((SLOTS, SLOTS), 0) == iota((SLOTS, SLOTS), 1))
    data_ref[:, 128:] = jnp.zeros((words * SLOTS, 128), jnp.bfloat16)
    total = jnp.zeros((1, 128), jnp.float32)
    for source, part, start in word_sources(in_refs, pos_ref[0]):
        here = pl.ds(pl.multiple_of(source * SLOTS, SLOTS), SLOTS)
        tail = part[start + SLOTS : start + SLOTS + EXTRA].astype(jnp.float32)
        rows = [jnp.concatenate([tail[2 * p : 2 * p + 1], tail[2 * p + 1 : 2 * p + 2]], axis=1) for p in range(4)]
        total = total + (tail[8:9] + tail[9:10] + tail[10:11])
        data_ref[here, :128] = part[start : start + SLOTS]
        data_ref[here, 128:144] = dot_nt(eye, stack_rows(rows, 16).astype(jnp.bfloat16)).astype(jnp.bfloat16)
    log_total = jnp.log(total)
    for t in range(n // 256):
        cut = slice(256 * t, 256 * t + 256)
        column = to_col(slot_ref[:, cut].astype(jnp.float32)).astype(jnp.int32)
        pick = dot_nn(one_hot(column == iota((256, words * SLOTS), 1)), data_ref[...])
        pick_ref[cut, :] = pick
        weight = to_row(pick[:, 128:129] + pick[:, 129:130] + pick[:, 130:131])
        on_diag = value_of(to_row(pick[:, 131:132]), log_total[:, :1], weight, weight)
        on_diag = on_diag.astype(jnp.bfloat16).astype(jnp.float32)
        stat_ref[:, cut] = stack_rows([weight, on_diag, jnp.broadcast_to(log_total[:, :1], (1, 256))], 8)
    first = pl.multiple_of(ctx * 128, 128)
    near = stat_ref[0:1, pl.ds(first, 128)]
    far = stat_ref[0:1, pl.ds(first + 1024, 128)]
    for t in range(n // 256):
        cut = slice(256 * t, 256 * t + 256)
        pick = pick_ref[cut, :]
        weight = pick[:, 128:129] + pick[:, 129:130] + pick[:, 130:131]
        gap = (iota((256, 128), 1) + ctx * 128 - iota((256, 128), 0) - 256 * t) & 2047
        other = jnp.where((gap >= 1) & (gap <= 1024), near, far)
        out_ref[cut, :] = value_of(pick[:, :128], log_total, weight, other).astype(jnp.bfloat16)


def own_kernel(pos_ref, slot_ref, stat_ref, weight_ref, *refs):
    in_refs, swapped_ref, out_ref = refs[:4], refs[4], refs[5]
    ctx = pos_ref[1]
    n = slot_ref.shape[1]
    out_rows, width = out_ref.shape[0], in_refs[0].shape[1]
    row_log = to_col(weight_ref[0:1])
    for t in range(n // 512):
        cut = slice(512 * t, 512 * t + 512)
        acc = jnp.zeros((out_rows, 512), jnp.float32)
        for r in range(8):
            source = ((ctx >> 1) - (r >> 1) & 3) * 2 + ((ctx ^ r) & 1)
            hot = one_hot(iota((width, 512), 0) + source * width == slot_ref[:, cut])
            step = r // 2
            part = swapped_ref[step * out_rows : (step + 1) * out_rows] if r % 2 else in_refs[step][:out_rows]
            acc += dot_nn(part, hot)
        out_ref[:, cut] = value_of(acc, stat_ref[2:3, cut], row_log, stat_ref[0:1, cut]).astype(jnp.bfloat16)


def move(value, step):
    return lax.ppermute(value, "ctx", [(c, (c + 2 * step) % 8) for c in range(8)])


def swap(value):
    return lax.ppermute(value, "ctx", [(c, c ^ 1) for c in range(8)])


def across(value, step):
    return lax.ppermute(value, "word", [(w, w // 4 * 4 + (w + step) % 4) for w in range(16)])


def along(value, step):
    return lax.ppermute(value, "word", [(w, (w + 4 * step) % 16) for w in range(16)])


def body(counts, row_totals, ctx_totals, samples):
    rows_dev, ctx_dev = counts.shape
    n_word = lax.axis_size("word")
    n_ctx = lax.axis_size("ctx")
    n = samples.shape[0]
    out_rows = rows_dev // n_ctx
    width = 2 * SLOTS
    pos = jnp.stack([lax.axis_index("word"), lax.axis_index("ctx")]).astype(jnp.int32)
    vmem = pl.BlockSpec(memory_space=pltpu.VMEM)
    smem = pl.BlockSpec(memory_space=pltpu.SMEM)
    half = jnp.bfloat16

    def whole(*shape):
        return pl.BlockSpec(shape, lambda g: (0,) * len(shape))

    *chunks, send, slot = pl.pallas_call(
        select_kernel,
        grid=(n_ctx // 2,),
        in_specs=[
            smem,
            whole(1, n),
            pl.BlockSpec((2 * out_rows, ctx_dev), lambda g: (g, 0)),
            whole(1, rows_dev),
            whole(1, ctx_dev),
        ],
        out_specs=[whole(2 * out_rows, width)] * 4 + [whole(n_ctx, SLOTS + EXTRA, 128), whole(1, n)],
        out_shape=[jax.ShapeDtypeStruct((2 * out_rows, width), half)] * 4
        + [
            jax.ShapeDtypeStruct((n_ctx, SLOTS + EXTRA, 128), half),
            jax.ShapeDtypeStruct((1, n), jnp.int32),
        ],
        scratch_shapes=[
            pltpu.VMEM((8, SLOTS), jnp.float32),
            pltpu.VMEM((ctx_dev, width), half),
            pltpu.VMEM((rows_dev, width), half),
        ],
        compiler_params=params(56),
    )(pos, samples.reshape(1, n), counts, row_totals.reshape(1, rows_dev), ctx_totals.reshape(1, ctx_dev))
    got = lax.all_to_all(send, "ctx", 0, 0, tiled=True)
    send, own_weight = pl.pallas_call(
        block_kernel,
        in_specs=[vmem] * 2,
        out_specs=[vmem, vmem],
        out_shape=[
            jax.ShapeDtypeStruct((SLOTS + EXTRA, 128), half),
            jax.ShapeDtypeStruct((8, 128), jnp.float32),
        ],
        compiler_params=params(16),
    )(row_totals.reshape(1, rows_dev), got)
    line = jnp.concatenate([send] + [across(send, step) for step in (1, -1, 2)], axis=0)
    left, right = along(line, 1), along(line, -1)
    middle = line.shape[0] // 2
    chunks, line = lax.optimization_barrier((chunks, line))
    mine = [chunks[0]] + [move(chunks[step], step) for step in (1, 2, 3)]
    lines = [line, left, right, along(left[:middle], 1), along(right[middle:], -1)]
    lines, mine = lax.optimization_barrier((lines, mine))
    part, stat = pl.pallas_call(
        core_kernel,
        in_specs=[smem] + [vmem] * 6,
        out_specs=[vmem, vmem],
        out_shape=[jax.ShapeDtypeStruct((n, 128), half), jax.ShapeDtypeStruct((8, n), jnp.float32)],
        scratch_shapes=[pltpu.VMEM((n_word * SLOTS, 256), half), pltpu.VMEM((n, 256), jnp.float32)],
        compiler_params=params(24),
    )(pos, slot, *lines)
    left, right = move(part, 1), move(part, -1)
    mine, part = lax.optimization_barrier((mine, part))
    swapped = swap(jnp.concatenate([value[out_rows:] for value in mine], axis=0))
    own = pl.pallas_call(
        own_kernel,
        in_specs=[smem] + [vmem] * 8,
        out_specs=vmem,
        out_shape=jax.ShapeDtypeStruct((out_rows, n), half),
        compiler_params=params(16),
        cost_estimate=pl.CostEstimate(flops=4 * out_rows * n * n, bytes_accessed=2 * MEGA, transcendentals=out_rows * n),
    )(pos, slot, stat, own_weight, *mine, swapped)
    left, right, own = lax.optimization_barrier((left, right, own))
    parts = [part, left, right, move(left[: n // 2], 1), move(right[n // 2 :], -1)]
    parts = parts + [swap(value) for value in parts]
    return factor(pos, parts, stat, own)


def solution(mesh):
    placed = (P("word", "ctx"), P("word"), P("ctx"), P())
    return jax.shard_map(
        body, mesh=mesh, in_specs=placed, out_specs=P(("word", "ctx"), None), check_vma=False
    )
```

```python
import math

import jax
import jax.numpy as jnp
from jax import lax
from jax.experimental import pallas as pl
from jax.experimental.pallas import tpu as pltpu
from jax.sharding import PartitionSpec as P

SAMPLES = 2048


NEG_LOG = math.log(5.0)


BLOCK = 256
SHIFT = 4.0 * math.sqrt(SAMPLES)
TOLERANCE = 1e-3
ROUNDS = (3, 2, 2, 2, 2, 2, 2, 3)


def dot_nn(left, right):
    return lax.dot_general(left, right, (((1,), (0,)), ((), ())), preferred_element_type=jnp.float32)


def dot_nt(left, right):
    return lax.dot_general(left, right, (((1,), (1,)), ((), ())), preferred_element_type=jnp.float32)


def exact_nt(left, right):
    return lax.dot_general(
        left, right, (((1,), (1,)), ((), ())), precision=lax.Precision.HIGHEST, preferred_element_type=jnp.float32
    )


def direct_factor(stat_ref, own_ref, core_ref, out_ref, tiles_ref, work_ref):
    count = core_ref.shape[0] // BLOCK
    out_rows = own_ref.shape[0]
    row_id = iota((BLOCK, 2 * BLOCK), 0)
    col_id = iota((BLOCK, 2 * BLOCK), 1)
    diag = iota((BLOCK, BLOCK), 0) == iota((BLOCK, BLOCK), 1)

    def span(i):
        return pl.ds(pl.multiple_of(i * BLOCK, BLOCK), BLOCK)

    def place(i, k):
        return i * (i - 1) // 2 + k

    def column(k, carry):
        block = core_ref[span(k), span(k)].astype(jnp.float32)
        block = jnp.where(diag, stat_ref[1:2, span(k)] + SHIFT, block)
        block = lax.fori_loop(
            0, k, lambda m, acc: acc - exact_nt(tiles_ref[place(k, m)], tiles_ref[place(k, m)]), block
        )
        work_ref[:, :BLOCK] = block
        work_ref[:, BLOCK:] = jnp.where(diag, 1.0, 0.0)

        def eliminate(j, carry):
            work = work_ref[...]
            row = jnp.sum(jnp.where(row_id == j, work, 0.0), axis=0, keepdims=True)
            col = jnp.sum(jnp.where(col_id == j, work, 0.0), axis=1, keepdims=True)
            pivot = jnp.sum(jnp.where(col_id[:1] == j, row, 0.0), axis=1, keepdims=True)
            scale = 1.0 / jnp.sqrt(pivot)
            row = row * scale
            work_ref[...] = jnp.where(row_id == j, row, jnp.where(row_id > j, work - (col * scale) * row, work))
            return carry

        lax.fori_loop(0, BLOCK, eliminate, 0)
        inv = work_ref[:, BLOCK:]

        def under(i, carry):
            tile = core_ref[span(i), span(k)].astype(jnp.float32)
            tile = lax.fori_loop(
                0, k, lambda m, acc: acc - exact_nt(tiles_ref[place(i, m)], tiles_ref[place(k, m)]), tile
            )
            tiles_ref[place(i, k)] = exact_nt(tile, inv)
            return carry

        lax.fori_loop(k + 1, count, under, 0)
        mine = own_ref[:, span(k)].astype(jnp.float32)
        mine = lax.fori_loop(
            0, k, lambda m, acc: acc - exact_nt(out_ref[:, span(m)], tiles_ref[place(k, m)]), mine
        )
        out_ref[:, span(k)] = exact_nt(mine, inv)
        return carry

    lax.fori_loop(0, count, column, 0)


def place_parts(refs, ctx, all_ref):
    for source, parts in sources(refs, ctx):
        lanes = pl.ds(pl.multiple_of(source * 128, 128), 128)
        start = 0
        for part in parts:
            all_ref[start : start + part.shape[0], lanes] = part[...]
            start += part.shape[0]


def factor_kernel(pos_ref, stat_ref, own_ref, *refs):
    part_refs, (out_ref, all_ref, core_ref, low_ref, tiles_ref, work_ref) = refs[:10], refs[10:]
    total = core_ref.shape[0]
    middle = total // 2
    half = jnp.bfloat16
    place_parts(part_refs, pos_ref[1], all_ref)
    row_id = iota((BLOCK, BLOCK), 0)
    col_id = iota((BLOCK, BLOCK), 1)
    diag = row_id == col_id
    below = row_id > col_id
    above = row_id < col_id
    eye = one_hot(diag)
    zero = jnp.zeros((BLOCK, BLOCK), half)

    def turned(tile):
        return dot_nt(eye, tile).astype(half)

    count = middle // BLOCK
    for i in range(count):
        for side in (0, middle):
            here = slice(side + i * BLOCK, side + (i + 1) * BLOCK)
            for j in range(i):
                core_ref[here, side + j * BLOCK : side + (j + 1) * BLOCK] = turned(
                    all_ref[side + j * BLOCK : side + (j + 1) * BLOCK, i * BLOCK : (i + 1) * BLOCK]
                )
            upper = jnp.where(above, all_ref[here, i * BLOCK : (i + 1) * BLOCK], zero)
            core_ref[here, here] = upper + turned(upper)
        here = slice(middle + i * BLOCK, middle + (i + 1) * BLOCK)
        for j in range(count):
            cols = slice(j * BLOCK, (j + 1) * BLOCK)
            if i > j:
                tile = all_ref[here, cols]
            else:
                tile = turned(all_ref[cols, i * BLOCK : (i + 1) * BLOCK])
            if i == j:
                tile = jnp.where(above, tile, all_ref[here, cols])
            core_ref[here, cols] = tile

    weight = jnp.where(below, 1.0, jnp.where(diag, 0.5, 0.0))
    worst = jnp.zeros((1, 1), jnp.float32)
    for k in range(total // BLOCK):
        lo, hi = k * BLOCK, (k + 1) * BLOCK
        block = core_ref[lo:hi, lo:hi].astype(jnp.float32)
        block = jnp.where(diag, stat_ref[1:2, lo:hi] + SHIFT, block)
        if k:
            pivot = low_ref[lo:hi, :lo]
            block = block - dot_nt(pivot, pivot)
        on_diag = jnp.where(diag, block, 0.0)
        scale_col = lax.rsqrt(jnp.sum(on_diag, axis=1, keepdims=True))
        scale_row = lax.rsqrt(jnp.sum(on_diag, axis=0, keepdims=True))
        off = jnp.where(diag, 0.0, block * scale_col * scale_row)
        step = off * weight
        inv = -step
        for _ in range(ROUNDS[k]):
            step_half = step.astype(half)
            inner = dot_nn(step_half, off.astype(half))
            off = dot_nt((inner + step - off).astype(half), step_half) - inner
            step = off * weight
            inv = inv - step - dot_nn(step.astype(half), inv.astype(half))
        worst = jnp.maximum(worst, jnp.sum(step * step, keepdims=True))
        inv_half = inv.astype(half)
        if hi < total:
            under = core_ref[hi:, lo:hi].astype(jnp.float32)
            if k:
                under = under - dot_nt(low_ref[hi:total, :lo], pivot)
            under = under * scale_row
            low_ref[hi:total, lo:hi] = (under + dot_nt(under.astype(half), inv_half)).astype(half)
        mine = own_ref[:, lo:hi].astype(jnp.float32)
        if k:
            mine = mine - dot_nt(low_ref[total:, :lo], pivot)
        mine = mine * scale_row
        mine = mine + dot_nt(mine.astype(half), inv_half)
        out_ref[:, lo:hi] = mine
        low_ref[total:, lo:hi] = mine.astype(half)

    @pl.when(jnp.logical_not(worst[0, 0] < TOLERANCE))
    def _():
        direct_factor(stat_ref, own_ref, core_ref, out_ref, tiles_ref, work_ref)


def factor(pos, parts, stat, own):
    out_rows, total = own.shape
    count = total // BLOCK
    vmem = pl.BlockSpec(memory_space=pltpu.VMEM)
    smem = pl.BlockSpec(memory_space=pltpu.SMEM)
    return pl.pallas_call(
        factor_kernel,
        out_shape=jax.ShapeDtypeStruct((out_rows, total), jnp.float32),
        in_specs=[smem] + [vmem] * 12,
        out_specs=vmem,
        scratch_shapes=[
            pltpu.VMEM((total, total // 2), jnp.bfloat16),
            pltpu.VMEM((total, total), jnp.bfloat16),
            pltpu.VMEM((total + out_rows, total), jnp.bfloat16),
            pltpu.VMEM((count * (count - 1) // 2, BLOCK, BLOCK), jnp.float32),
            pltpu.VMEM((BLOCK, 2 * BLOCK), jnp.float32),
        ],
        compiler_params=params(40),
    )(pos, stat, own, *parts)


SLOTS = 256
EXTRA = 16
MEGA = 1024 * 1024


def params(limit=48):
    return pltpu.CompilerParams(vmem_limit_bytes=limit * MEGA)


def iota(shape, dim):
    return lax.broadcasted_iota(jnp.int32, shape, dim)


def to_col(row):
    n = row.shape[1]
    square = iota((n, n), 0) == iota((n, n), 1)
    return jnp.sum(jnp.where(square, jnp.broadcast_to(row, (n, n)), 0.0), axis=1, keepdims=True)


def to_row(col):
    n = col.shape[0]
    square = iota((n, n), 0) == iota((n, n), 1)
    return jnp.sum(jnp.where(square, jnp.broadcast_to(col, (n, n)), 0.0), axis=0, keepdims=True)


def stack_rows(rows, height):
    width = rows[0].shape[1]
    index = iota((height, width), 0)
    out = jnp.zeros((height, width), jnp.float32)
    for r, row in enumerate(rows):
        out = jnp.where(index == r, jnp.broadcast_to(row, (height, width)), out)
    return out


def one_hot(mask):
    return jnp.where(mask, 1.0, 0.0).astype(jnp.bfloat16)


def pieces(value):
    high = value.astype(jnp.bfloat16).astype(jnp.float32)
    rest = value - high
    middle = rest.astype(jnp.bfloat16).astype(jnp.float32)
    return [high, middle, rest - middle]


def select_kernel(pos_ref, small_ref, counts_hbm, *refs):
    chunk_refs, (send_ref, slot_ref, index_ref, hot_ref, picked_ref) = refs[:5], refs[5:10]
    counts_ref, sems = refs[10:]
    word, ctx = pos_ref[0], pos_ref[1]
    n = slot_ref.shape[1]
    width = hot_ref.shape[1]
    share = chunk_refs[0].shape[0]
    rows = 2 * share
    steps = counts_ref.shape[0] // rows
    copies = []
    for g in range(steps):
        cut = slice(g * rows, (g + 1) * rows)
        copies.append(pltpu.make_async_copy(counts_hbm.at[cut], counts_ref.at[cut], sems.at[g]))
        copies[g].start()

    sample = small_ref[:, :n]
    block = sample >> 10
    member = jnp.where(iota((16, n), 0) == block, 1.0, 0.0)
    before = one_hot(iota((256, 256), 0) < iota((256, 256), 1))
    count = jnp.zeros((16, 1), jnp.float32)
    k = iota((1, n), 1)
    local = sample & 2047
    vals = stack_rows(
        [v.astype(jnp.float32) for v in (local >> 8, local & 255, local * 0 + 1, k >> 8, k & 255, (local & 1023) >> 8)],
        8,
    ).astype(jnp.bfloat16)
    by_ctx = jnp.zeros((8, width), jnp.float32)
    by_word = jnp.zeros((8, SLOTS), jnp.float32)
    for t in range(n // 256):
        cut = slice(256 * t, 256 * t + 256)
        mine = member[:, cut]
        rank = dot_nn(mine.astype(jnp.bfloat16), before) + count
        count = count + jnp.sum(mine, axis=1, keepdims=True)
        slot = block[:, cut].astype(jnp.float32) * SLOTS + jnp.sum(mine * rank, axis=0, keepdims=True)
        slot_ref[:, cut] = slot.astype(jnp.int32)
        column = to_col(slot).astype(jnp.int32)
        by_ctx += dot_nn(vals[:, cut], one_hot(column - ctx * width == iota((256, width), 1)))
        by_word += dot_nn(vals[:, cut], one_hot(column - word * SLOTS == iota((256, SLOTS), 1)))
    col = jnp.where(by_ctx[2:3] > 0, by_ctx[0:1] * 256 + by_ctx[1:2], -1.0).astype(jnp.int32)
    for t in range(hot_ref.shape[0] // 256):
        hot_ref[256 * t : 256 * t + 256] = one_hot(iota((256, width), 0) + 256 * t == col)
    row = jnp.where(by_word[2:3] > 0, by_word[5:6] * 256 + by_word[1:2], -1.0)
    index_ref[...] = stack_rows([row, by_word[3:4] * 256 + by_word[4:5]], 8)

    for g in range(steps):
        copies[g].wait()
        cut = slice(g * rows, (g + 1) * rows)
        chunk = dot_nn(counts_ref[cut].astype(jnp.float32).astype(jnp.bfloat16), hot_ref[...]).astype(jnp.bfloat16)
        picked_ref[cut] = chunk
        odd = (ctx & 1) == 1
        same = jnp.where(odd, chunk[share:], chunk[:share])
        other = jnp.where(odd, chunk[:share], chunk[share:])
        for r in range(steps):

            @pl.when((g - (ctx >> 1) & 3) == r)
            def _(r=r, same=same, other=other):
                if r == 0:
                    chunk_refs[0][...] = same
                    chunk_refs[1][...] = other
                else:
                    chunk_refs[1 + r][:share] = same
                    chunk_refs[1 + r][share:] = other

    total_rows = picked_ref.shape[0]
    row_hot = one_hot(to_col(index_ref[0:1]).astype(jnp.int32) == iota((SLOTS, total_rows), 1))
    picked = dot_nn(row_hot, picked_ref[...])
    tile = jnp.where((word & 1) == 1, picked[:, SLOTS:], picked[:, :SLOTS])
    square = iota((SLOTS, SLOTS), 0) == iota((SLOTS, SLOTS), 1)
    own_diag = jnp.sum(jnp.where(square, tile, 0.0), axis=0, keepdims=True)
    here = small_ref[:, pl.ds(pl.multiple_of(n + total_rows + (word & 1) * total_rows, total_rows), total_rows)]
    weight = 0.5 * (jnp.log(small_ref[:, n : n + total_rows].astype(jnp.float32)) + jnp.log(here.astype(jnp.float32)))
    weight_parts = pieces(weight)
    slot_weight = dot_nt(stack_rows(weight_parts, 16).astype(jnp.bfloat16), row_hot)
    parts = []
    for p in range(3):
        parts += [slot_weight[p : p + 1, :128], slot_weight[p : p + 1, 128:]]
    parts += [own_diag[:, :128], own_diag[:, 128:]]
    holder = ctx == word >> 1
    full = dot_nn(
        picked.astype(jnp.bfloat16), one_hot(iota((width, n), 0) + ctx * width == slot_ref[...])
    )
    k_col = to_col(index_ref[1:2]).astype(jnp.int32)
    gap = (iota((SLOTS, n // 2), 1) - k_col) & (n - 1)
    head = jnp.where((gap >= 1) & (gap <= n // 2), full[:, : n // 2], full[:, n // 2 :]).astype(jnp.bfloat16)
    for c in range(8):
        lanes = slice(128 * c, 128 * c + 128)
        tail = stack_rows(parts + [p[:, lanes] for p in weight_parts], EXTRA)
        send_ref[c, :SLOTS] = head[:, lanes]
        send_ref[c, SLOTS:] = jnp.where(holder, tail, 0.0).astype(jnp.bfloat16)


def sources(refs, ctx):
    z, core = ctx >> 1, ctx & 1
    out = []
    for half in (0, 1):
        own, left, right, top, bottom = refs[5 * half : 5 * half + 5]
        for step, parts in ((0, (own,)), (3, (left,)), (1, (right,)), (2, (top, bottom))):
            out.append((((z + step) & 3) * 2 + (core ^ half), parts))
    return out


def block_kernel(totals_ref, got_ref, send_ref, own_ref):
    got = got_ref[0].astype(jnp.float32)
    for c in range(1, got_ref.shape[0]):
        got = got + got_ref[c].astype(jnp.float32)
    tail = got[SLOTS:]
    own_ref[...] = jnp.broadcast_to(tail[8:9] + tail[9:10] + tail[10:11], own_ref.shape)
    total = pieces(jnp.sum(totals_ref[...].astype(jnp.float32), axis=1, keepdims=True))
    row = iota(tail.shape, 0)
    for p in range(3):
        tail = jnp.where(row == 8 + p, jnp.broadcast_to(total[p], tail.shape), tail)
    send_ref[:SLOTS] = got[:SLOTS].astype(jnp.bfloat16)
    send_ref[SLOTS:] = tail.astype(jnp.bfloat16)


def value_of(count, log_total, row_log, col_log):
    value = jnp.log(jnp.maximum(count, 1.0)) + log_total - row_log - col_log - NEG_LOG
    return jnp.where(count > 0, jnp.maximum(value, 0.0), 0.0)


def word_sources(refs, word):
    y, x = word >> 2, word & 3
    own, left, right, top, bottom = refs
    for step, parts in ((0, (own,)), (3, (left,)), (1, (right,)), (2, (top, bottom))):
        for i, across in enumerate((0, 3, 1, 2)):
            part, place = (parts[0], i) if len(parts) == 1 else (parts[i // 2], i % 2)
            yield ((y + step) & 3) * 4 + ((x + across) & 3), part, place * (SLOTS + EXTRA)


def core_kernel(pos_ref, slot_ref, *refs):
    in_refs, (out_ref, stat_ref, data_ref, pick_ref) = refs[:5], refs[5:]
    ctx = pos_ref[1]
    n = slot_ref.shape[1]
    words = data_ref.shape[0] // SLOTS
    eye = one_hot(iota((SLOTS, SLOTS), 0) == iota((SLOTS, SLOTS), 1))
    data_ref[:, 128:] = jnp.zeros((words * SLOTS, 128), jnp.bfloat16)
    total = jnp.zeros((1, 128), jnp.float32)
    for source, part, start in word_sources(in_refs, pos_ref[0]):
        here = pl.ds(pl.multiple_of(source * SLOTS, SLOTS), SLOTS)
        tail = part[start + SLOTS : start + SLOTS + EXTRA].astype(jnp.float32)
        rows = [jnp.concatenate([tail[2 * p : 2 * p + 1], tail[2 * p + 1 : 2 * p + 2]], axis=1) for p in range(4)]
        total = total + (tail[8:9] + tail[9:10] + tail[10:11])
        data_ref[here, :128] = part[start : start + SLOTS]
        data_ref[here, 128:144] = dot_nt(eye, stack_rows(rows, 16).astype(jnp.bfloat16)).astype(jnp.bfloat16)
    log_total = jnp.log(total)
    for t in range(n // 256):
        cut = slice(256 * t, 256 * t + 256)
        column = to_col(slot_ref[:, cut].astype(jnp.float32)).astype(jnp.int32)
        pick = dot_nn(one_hot(column == iota((256, words * SLOTS), 1)), data_ref[...])
        pick_ref[cut, :] = pick
        weight = to_row(pick[:, 128:129] + pick[:, 129:130] + pick[:, 130:131])
        on_diag = value_of(to_row(pick[:, 131:132]), log_total[:, :1], weight, weight)
        on_diag = on_diag.astype(jnp.bfloat16).astype(jnp.float32)
        stat_ref[:, cut] = stack_rows([weight, on_diag, jnp.broadcast_to(log_total[:, :1], (1, 256))], 8)
    first = pl.multiple_of(ctx * 128, 128)
    near = stat_ref[0:1, pl.ds(first, 128)]
    far = stat_ref[0:1, pl.ds(first + 1024, 128)]
    for t in range(n // 256):
        cut = slice(256 * t, 256 * t + 256)
        pick = pick_ref[cut, :]
        weight = pick[:, 128:129] + pick[:, 129:130] + pick[:, 130:131]
        gap = (iota((256, 128), 1) + ctx * 128 - iota((256, 128), 0) - 256 * t) & 2047
        other = jnp.where((gap >= 1) & (gap <= 1024), near, far)
        out_ref[cut, :] = value_of(pick[:, :128], log_total, weight, other).astype(jnp.bfloat16)


def own_kernel(pos_ref, slot_ref, stat_ref, weight_ref, *refs):
    in_refs, swapped_ref, out_ref = refs[:4], refs[4], refs[5]
    ctx = pos_ref[1]
    n = slot_ref.shape[1]
    out_rows, width = out_ref.shape[0], in_refs[0].shape[1]
    row_log = to_col(weight_ref[0:1])
    for t in range(n // 512):
        cut = slice(512 * t, 512 * t + 512)
        acc = jnp.zeros((out_rows, 512), jnp.float32)
        for r in range(8):
            source = ((ctx >> 1) - (r >> 1) & 3) * 2 + ((ctx ^ r) & 1)
            hot = one_hot(iota((width, 512), 0) + source * width == slot_ref[:, cut])
            step = r // 2
            part = swapped_ref[step * out_rows : (step + 1) * out_rows] if r % 2 else in_refs[step][:out_rows]
            acc += dot_nn(part, hot)
        out_ref[:, cut] = value_of(acc, stat_ref[2:3, cut], row_log, stat_ref[0:1, cut]).astype(jnp.bfloat16)


def move(value, step):
    return lax.ppermute(value, "ctx", [(c, (c + 2 * step) % 8) for c in range(8)])


def swap(value):
    return lax.ppermute(value, "ctx", [(c, c ^ 1) for c in range(8)])


def across(value, step):
    return lax.ppermute(value, "word", [(w, w // 4 * 4 + (w + step) % 4) for w in range(16)])


def along(value, step):
    return lax.ppermute(value, "word", [(w, (w + 4 * step) % 16) for w in range(16)])


def body(counts, row_totals, ctx_totals, samples):
    rows_dev, ctx_dev = counts.shape
    n_word = lax.axis_size("word")
    n_ctx = lax.axis_size("ctx")
    n = samples.shape[0]
    out_rows = rows_dev // n_ctx
    width = 2 * SLOTS
    pos = jnp.stack([lax.axis_index("word"), lax.axis_index("ctx")]).astype(jnp.int32)
    vmem = pl.BlockSpec(memory_space=pltpu.VMEM)
    smem = pl.BlockSpec(memory_space=pltpu.SMEM)
    half = jnp.bfloat16

    hbm = pl.BlockSpec(memory_space=pltpu.HBM)
    *chunks, send, slot = pl.pallas_call(
        select_kernel,
        in_specs=[smem, vmem, hbm],
        out_specs=[vmem] * 7,
        out_shape=[jax.ShapeDtypeStruct((out_rows, width), half)] * 2
        + [jax.ShapeDtypeStruct((2 * out_rows, width), half)] * 3
        + [
            jax.ShapeDtypeStruct((n_ctx, SLOTS + EXTRA, 128), half),
            jax.ShapeDtypeStruct((1, n), jnp.int32),
        ],
        scratch_shapes=[
            pltpu.VMEM((8, SLOTS), jnp.float32),
            pltpu.VMEM((ctx_dev, width), half),
            pltpu.VMEM((rows_dev, width), half),
            pltpu.VMEM((rows_dev, ctx_dev), jnp.int32),
            pltpu.SemaphoreType.DMA((4,)),
        ],
        compiler_params=params(52),
    )(pos, jnp.concatenate([samples, row_totals, ctx_totals]).reshape(1, n + rows_dev + ctx_dev), counts)
    got = lax.all_to_all(send, "ctx", 0, 0, tiled=True)
    send, own_weight = pl.pallas_call(
        block_kernel,
        in_specs=[vmem] * 2,
        out_specs=[vmem, vmem],
        out_shape=[
            jax.ShapeDtypeStruct((SLOTS + EXTRA, 128), half),
            jax.ShapeDtypeStruct((8, 128), jnp.float32),
        ],
        compiler_params=params(16),
    )(row_totals.reshape(1, rows_dev), got)
    line = jnp.concatenate([send] + [across(send, step) for step in (1, -1, 2)], axis=0)
    left, right = along(line, 1), along(line, -1)
    middle = line.shape[0] // 2
    chunks, line = lax.optimization_barrier((chunks, line))
    mine = chunks[:2] + [move(chunks[1 + step], step) for step in (1, 2, 3)]
    lines = [line, left, right, along(left[:middle], 1), along(right[middle:], -1)]
    lines, mine = lax.optimization_barrier((lines, mine))
    part, stat = pl.pallas_call(
        core_kernel,
        in_specs=[smem] + [vmem] * 6,
        out_specs=[vmem, vmem],
        out_shape=[jax.ShapeDtypeStruct((n, 128), half), jax.ShapeDtypeStruct((8, n), jnp.float32)],
        scratch_shapes=[pltpu.VMEM((n_word * SLOTS, 256), half), pltpu.VMEM((n, 256), jnp.float32)],
        compiler_params=params(24),
    )(pos, slot, *lines)
    left, right = move(part, 1), move(part, -1)
    mine, part = lax.optimization_barrier((mine, part))
    swapped = swap(jnp.concatenate([mine[1]] + [value[out_rows:] for value in mine[2:]], axis=0))
    own = pl.pallas_call(
        own_kernel,
        in_specs=[smem] + [vmem] * 8,
        out_specs=vmem,
        out_shape=jax.ShapeDtypeStruct((out_rows, n), half),
        compiler_params=params(16),
        cost_estimate=pl.CostEstimate(flops=4 * out_rows * n * n, bytes_accessed=2 * MEGA, transcendentals=out_rows * n),
    )(pos, slot, stat, own_weight, mine[0], *mine[2:], swapped)
    left, right, own = lax.optimization_barrier((left, right, own))
    parts = [part, left, right, move(left[: n // 2], 1), move(right[n // 2 :], -1)]
    parts = parts + [swap(value) for value in parts]
    return factor(pos, parts, stat, own)


def solution(mesh):
    placed = (P("word", "ctx"), P("word"), P("ctx"), P())
    return jax.shard_map(
        body, mesh=mesh, in_specs=placed, out_specs=P(("word", "ctx"), None), check_vma=False
    )
```

```python
import math

import jax
import jax.numpy as jnp
from jax import lax
from jax.experimental import pallas as pl
from jax.experimental.pallas import tpu as pltpu
from jax.sharding import PartitionSpec as P

SAMPLES = 2048


NEG_LOG = math.log(5.0)


BLOCK = 256
SHIFT = 4.0 * math.sqrt(SAMPLES)
TOLERANCE = 1e-3
ROUNDS = (3, 2, 2, 2, 2, 2, 2, 3)


def dot_nn(left, right):
    return lax.dot_general(left, right, (((1,), (0,)), ((), ())), preferred_element_type=jnp.float32)


def dot_nt(left, right):
    return lax.dot_general(left, right, (((1,), (1,)), ((), ())), preferred_element_type=jnp.float32)


def exact_nt(left, right):
    return lax.dot_general(
        left, right, (((1,), (1,)), ((), ())), precision=lax.Precision.HIGHEST, preferred_element_type=jnp.float32
    )


def direct_factor(stat_ref, own_ref, core_ref, out_ref, tiles_ref, work_ref):
    count = core_ref.shape[1] // BLOCK
    out_rows = own_ref.shape[0]
    row_id = iota((BLOCK, 2 * BLOCK), 0)
    col_id = iota((BLOCK, 2 * BLOCK), 1)
    diag = iota((BLOCK, BLOCK), 0) == iota((BLOCK, BLOCK), 1)

    def span(i):
        return pl.ds(pl.multiple_of(i * BLOCK, BLOCK), BLOCK)

    def place(i, k):
        return i * (i - 1) // 2 + k

    def column(k, carry):
        block = core_ref[span(k), span(k)].astype(jnp.float32)
        block = jnp.where(diag, stat_ref[1:2, span(k)] + SHIFT, block)
        block = lax.fori_loop(
            0, k, lambda m, acc: acc - exact_nt(tiles_ref[place(k, m)], tiles_ref[place(k, m)]), block
        )
        work_ref[:, :BLOCK] = block
        work_ref[:, BLOCK:] = jnp.where(diag, 1.0, 0.0)

        def eliminate(j, carry):
            work = work_ref[...]
            row = jnp.sum(jnp.where(row_id == j, work, 0.0), axis=0, keepdims=True)
            col = jnp.sum(jnp.where(col_id == j, work, 0.0), axis=1, keepdims=True)
            pivot = jnp.sum(jnp.where(col_id[:1] == j, row, 0.0), axis=1, keepdims=True)
            scale = 1.0 / jnp.sqrt(pivot)
            row = row * scale
            work_ref[...] = jnp.where(row_id == j, row, jnp.where(row_id > j, work - (col * scale) * row, work))
            return carry

        lax.fori_loop(0, BLOCK, eliminate, 0)
        inv = work_ref[:, BLOCK:]

        def under(i, carry):
            tile = core_ref[span(i), span(k)].astype(jnp.float32)
            tile = lax.fori_loop(
                0, k, lambda m, acc: acc - exact_nt(tiles_ref[place(i, m)], tiles_ref[place(k, m)]), tile
            )
            tiles_ref[place(i, k)] = exact_nt(tile, inv)
            return carry

        lax.fori_loop(k + 1, count, under, 0)
        mine = own_ref[:, span(k)].astype(jnp.float32)
        mine = lax.fori_loop(
            0, k, lambda m, acc: acc - exact_nt(out_ref[:, span(m)], tiles_ref[place(k, m)]), mine
        )
        out_ref[:, span(k)] = exact_nt(mine, inv)
        return carry

    lax.fori_loop(0, count, column, 0)


def place_parts(refs, ctx, all_ref):
    for source, parts in sources(refs, ctx):
        lanes = pl.ds(pl.multiple_of(source * 128, 128), 128)
        start = 0
        for part in parts:
            all_ref[start : start + part.shape[0], lanes] = part[...]
            start += part.shape[0]


def factor_kernel(pos_ref, stat_ref, own_ref, *refs):
    part_refs, (out_ref, all_ref, core_ref, low_ref, tiles_ref, work_ref) = refs[:10], refs[10:]
    total = core_ref.shape[1]
    middle = total // 2
    half = jnp.bfloat16
    place_parts(part_refs, pos_ref[1], all_ref)
    core_ref[total:] = own_ref[...]
    row_id = iota((BLOCK, BLOCK), 0)
    col_id = iota((BLOCK, BLOCK), 1)
    diag = row_id == col_id
    below = row_id > col_id
    above = row_id < col_id
    eye = one_hot(diag)
    zero = jnp.zeros((BLOCK, BLOCK), half)

    def turned(tile):
        return dot_nt(eye, tile).astype(half)

    count = middle // BLOCK
    for i in range(count):
        for side in (0, middle):
            here = slice(side + i * BLOCK, side + (i + 1) * BLOCK)
            for j in range(i):
                core_ref[here, side + j * BLOCK : side + (j + 1) * BLOCK] = turned(
                    all_ref[side + j * BLOCK : side + (j + 1) * BLOCK, i * BLOCK : (i + 1) * BLOCK]
                )
            upper = jnp.where(above, all_ref[here, i * BLOCK : (i + 1) * BLOCK], zero)
            core_ref[here, here] = upper + turned(upper)
        here = slice(middle + i * BLOCK, middle + (i + 1) * BLOCK)
        for j in range(count):
            cols = slice(j * BLOCK, (j + 1) * BLOCK)
            if i > j:
                tile = all_ref[here, cols]
            else:
                tile = turned(all_ref[cols, i * BLOCK : (i + 1) * BLOCK])
            if i == j:
                tile = jnp.where(above, tile, all_ref[here, cols])
            core_ref[here, cols] = tile

    weight = jnp.where(below, 1.0, jnp.where(diag, 0.5, 0.0))
    worst = jnp.zeros((1, 1), jnp.float32)
    for k in range(total // BLOCK):
        lo, hi = k * BLOCK, (k + 1) * BLOCK
        block = core_ref[lo:hi, lo:hi].astype(jnp.float32)
        block = jnp.where(diag, stat_ref[1:2, lo:hi] + SHIFT, block)
        if k:
            pivot = low_ref[lo:hi, :lo]
            block = block - dot_nt(pivot, pivot)
        on_diag = jnp.where(diag, block, 0.0)
        scale_col = lax.rsqrt(jnp.sum(on_diag, axis=1, keepdims=True))
        scale_row = lax.rsqrt(jnp.sum(on_diag, axis=0, keepdims=True))
        off = jnp.where(diag, 0.0, block * scale_col * scale_row)
        step = off * weight
        inv = -step
        for _ in range(ROUNDS[k]):
            step_half = step.astype(half)
            inner = dot_nn(step_half, off.astype(half))
            off = dot_nt((inner + step - off).astype(half), step_half) - inner
            step = off * weight
            inv = inv - step - dot_nn(step.astype(half), inv.astype(half))
        worst = jnp.maximum(worst, jnp.sum(step * step, keepdims=True))
        inv_half = inv.astype(half)
        under = core_ref[hi:, lo:hi].astype(jnp.float32)
        if k:
            under = under - dot_nt(low_ref[hi:, :lo], pivot)
        under = under * scale_row
        under = under + dot_nt(under.astype(half), inv_half)
        low_ref[hi:, lo:hi] = under.astype(half)
        out_ref[:, lo:hi] = under[total - hi :]

    @pl.when(jnp.logical_not(worst[0, 0] < TOLERANCE))
    def _():
        direct_factor(stat_ref, own_ref, core_ref, out_ref, tiles_ref, work_ref)


def factor(pos, parts, stat, own):
    out_rows, total = own.shape
    count = total // BLOCK
    vmem = pl.BlockSpec(memory_space=pltpu.VMEM)
    smem = pl.BlockSpec(memory_space=pltpu.SMEM)
    return pl.pallas_call(
        factor_kernel,
        out_shape=jax.ShapeDtypeStruct((out_rows, total), jnp.float32),
        in_specs=[smem] + [vmem] * 12,
        out_specs=vmem,
        scratch_shapes=[
            pltpu.VMEM((total, total // 2), jnp.bfloat16),
            pltpu.VMEM((total + out_rows, total), jnp.bfloat16),
            pltpu.VMEM((total + out_rows, total), jnp.bfloat16),
            pltpu.VMEM((count * (count - 1) // 2, BLOCK, BLOCK), jnp.float32),
            pltpu.VMEM((BLOCK, 2 * BLOCK), jnp.float32),
        ],
        compiler_params=params(40),
    )(pos, stat, own, *parts)


SLOTS = 256
EXTRA = 16
MEGA = 1024 * 1024


def params(limit=48):
    return pltpu.CompilerParams(vmem_limit_bytes=limit * MEGA)


def iota(shape, dim):
    return lax.broadcasted_iota(jnp.int32, shape, dim)


def to_col(row):
    n = row.shape[1]
    square = iota((n, n), 0) == iota((n, n), 1)
    return jnp.sum(jnp.where(square, jnp.broadcast_to(row, (n, n)), 0.0), axis=1, keepdims=True)


def to_row(col):
    n = col.shape[0]
    square = iota((n, n), 0) == iota((n, n), 1)
    return jnp.sum(jnp.where(square, jnp.broadcast_to(col, (n, n)), 0.0), axis=0, keepdims=True)


def stack_rows(rows, height):
    width = rows[0].shape[1]
    index = iota((height, width), 0)
    out = jnp.zeros((height, width), jnp.float32)
    for r, row in enumerate(rows):
        out = jnp.where(index == r, jnp.broadcast_to(row, (height, width)), out)
    return out


def one_hot(mask):
    return jnp.where(mask, 1.0, 0.0).astype(jnp.bfloat16)


def pieces(value):
    high = value.astype(jnp.bfloat16).astype(jnp.float32)
    rest = value - high
    middle = rest.astype(jnp.bfloat16).astype(jnp.float32)
    return [high, middle, rest - middle]


def select_kernel(pos_ref, small_ref, counts_hbm, *refs):
    chunk_refs, (send_ref, slot_ref, index_ref, hot_ref, picked_ref) = refs[:5], refs[5:10]
    counts_ref, sems = refs[10:]
    word, ctx = pos_ref[0], pos_ref[1]
    n = slot_ref.shape[1]
    width = hot_ref.shape[1]
    share = chunk_refs[0].shape[0]
    rows = 2 * share
    steps = counts_ref.shape[0] // rows
    copies = []
    for g in range(steps):
        cut = slice(g * rows, (g + 1) * rows)
        copies.append(pltpu.make_async_copy(counts_hbm.at[cut], counts_ref.at[cut], sems.at[g]))
        copies[g].start()

    sample = small_ref[:, :n]
    block = sample >> 10
    member = jnp.where(iota((16, n), 0) == block, 1.0, 0.0)
    before = one_hot(iota((256, 256), 0) < iota((256, 256), 1))
    count = jnp.zeros((16, 1), jnp.float32)
    k = iota((1, n), 1)
    local = sample & 2047
    vals = stack_rows(
        [v.astype(jnp.float32) for v in (local >> 8, local & 255, local * 0 + 1, k >> 8, k & 255, (local & 1023) >> 8)],
        8,
    ).astype(jnp.bfloat16)
    by_ctx = jnp.zeros((8, width), jnp.float32)
    by_word = jnp.zeros((8, SLOTS), jnp.float32)
    for t in range(n // 256):
        cut = slice(256 * t, 256 * t + 256)
        mine = member[:, cut]
        rank = dot_nn(mine.astype(jnp.bfloat16), before) + count
        count = count + jnp.sum(mine, axis=1, keepdims=True)
        slot = block[:, cut].astype(jnp.float32) * SLOTS + jnp.sum(mine * rank, axis=0, keepdims=True)
        slot_ref[:, cut] = slot.astype(jnp.int32)
        column = to_col(slot).astype(jnp.int32)
        by_ctx += dot_nn(vals[:, cut], one_hot(column - ctx * width == iota((256, width), 1)))
        by_word += dot_nn(vals[:, cut], one_hot(column - word * SLOTS == iota((256, SLOTS), 1)))
    col = jnp.where(by_ctx[2:3] > 0, by_ctx[0:1] * 256 + by_ctx[1:2], -1.0).astype(jnp.int32)
    for t in range(hot_ref.shape[0] // 256):
        hot_ref[256 * t : 256 * t + 256] = one_hot(iota((256, width), 0) + 256 * t == col)
    row = jnp.where(by_word[2:3] > 0, by_word[5:6] * 256 + by_word[1:2], -1.0)
    index_ref[...] = stack_rows([row, by_word[3:4] * 256 + by_word[4:5]], 8)

    for g in range(steps):
        if g % 2 == 0:
            copies[g].wait()
            copies[g + 1].wait()
            cut = slice(g * rows, (g + 2) * rows)
            pair = counts_ref[cut].astype(jnp.float32).astype(jnp.bfloat16)
            pair = dot_nn(pair, hot_ref[...]).astype(jnp.bfloat16)
            picked_ref[cut] = pair
        chunk = pair[g % 2 * rows : (g % 2 + 1) * rows]
        odd = (ctx & 1) == 1
        same = jnp.where(odd, chunk[share:], chunk[:share])
        other = jnp.where(odd, chunk[:share], chunk[share:])
        for r in range(steps):

            @pl.when((g - (ctx >> 1) & 3) == r)
            def _(r=r, same=same, other=other):
                if r == 0:
                    chunk_refs[0][...] = same
                    chunk_refs[1][...] = other
                else:
                    chunk_refs[1 + r][:share] = same
                    chunk_refs[1 + r][share:] = other

    total_rows = picked_ref.shape[0]
    row_hot = one_hot(to_col(index_ref[0:1]).astype(jnp.int32) == iota((SLOTS, total_rows), 1))
    picked = dot_nn(row_hot, picked_ref[...])
    tile = jnp.where((word & 1) == 1, picked[:, SLOTS:], picked[:, :SLOTS])
    square = iota((SLOTS, SLOTS), 0) == iota((SLOTS, SLOTS), 1)
    own_diag = jnp.sum(jnp.where(square, tile, 0.0), axis=0, keepdims=True)
    here = small_ref[:, pl.ds(pl.multiple_of(n + total_rows + (word & 1) * total_rows, total_rows), total_rows)]
    weight = 0.5 * (jnp.log(small_ref[:, n : n + total_rows].astype(jnp.float32)) + jnp.log(here.astype(jnp.float32)))
    weight_parts = pieces(weight)
    slot_weight = dot_nt(stack_rows(weight_parts, 16).astype(jnp.bfloat16), row_hot)
    parts = []
    for p in range(3):
        parts += [slot_weight[p : p + 1, :128], slot_weight[p : p + 1, 128:]]
    parts += [own_diag[:, :128], own_diag[:, 128:]]
    holder = ctx == word >> 1
    full = dot_nn(
        picked.astype(jnp.bfloat16), one_hot(iota((width, n), 0) + ctx * width == slot_ref[...])
    )
    k_col = to_col(index_ref[1:2]).astype(jnp.int32)
    gap = (iota((SLOTS, n // 2), 1) - k_col) & (n - 1)
    head = jnp.where((gap >= 1) & (gap <= n // 2), full[:, : n // 2], full[:, n // 2 :]).astype(jnp.bfloat16)
    for c in range(8):
        lanes = slice(128 * c, 128 * c + 128)
        tail = stack_rows(parts + [p[:, lanes] for p in weight_parts], EXTRA)
        send_ref[c, :SLOTS] = head[:, lanes]
        send_ref[c, SLOTS:] = jnp.where(holder, tail, 0.0).astype(jnp.bfloat16)


def sources(refs, ctx):
    z, core = ctx >> 1, ctx & 1
    out = []
    for half in (0, 1):
        own, left, right, top, bottom = refs[5 * half : 5 * half + 5]
        for step, parts in ((0, (own,)), (3, (left,)), (1, (right,)), (2, (top, bottom))):
            out.append((((z + step) & 3) * 2 + (core ^ half), parts))
    return out


def block_kernel(totals_ref, got_ref, send_ref, own_ref):
    got = got_ref[0].astype(jnp.float32)
    for c in range(1, got_ref.shape[0]):
        got = got + got_ref[c].astype(jnp.float32)
    tail = got[SLOTS:]
    own_ref[...] = jnp.broadcast_to(tail[8:9] + tail[9:10] + tail[10:11], own_ref.shape)
    total = pieces(jnp.sum(totals_ref[...].astype(jnp.float32), axis=1, keepdims=True))
    row = iota(tail.shape, 0)
    for p in range(3):
        tail = jnp.where(row == 8 + p, jnp.broadcast_to(total[p], tail.shape), tail)
    send_ref[:SLOTS] = got[:SLOTS].astype(jnp.bfloat16)
    send_ref[SLOTS:] = tail.astype(jnp.bfloat16)


def value_of(count, log_total, row_log, col_log):
    value = jnp.log(jnp.maximum(count, 1.0)) + log_total - row_log - col_log - NEG_LOG
    return jnp.where(count > 0, jnp.maximum(value, 0.0), 0.0)


def word_sources(refs, word):
    y, x = word >> 2, word & 3
    own, left, right, top, bottom = refs
    for step, parts in ((0, (own,)), (3, (left,)), (1, (right,)), (2, (top, bottom))):
        for i, across in enumerate((0, 3, 1, 2)):
            part, place = (parts[0], i) if len(parts) == 1 else (parts[i // 2], i % 2)
            yield ((y + step) & 3) * 4 + ((x + across) & 3), part, place * (SLOTS + EXTRA)


def core_kernel(pos_ref, slot_ref, *refs):
    in_refs, (out_ref, stat_ref, data_ref, pick_ref) = refs[:5], refs[5:]
    ctx = pos_ref[1]
    n = slot_ref.shape[1]
    words = data_ref.shape[0] // SLOTS
    eye = one_hot(iota((SLOTS, SLOTS), 0) == iota((SLOTS, SLOTS), 1))
    data_ref[:, 128:] = jnp.zeros((words * SLOTS, 128), jnp.bfloat16)
    total = jnp.zeros((1, 128), jnp.float32)
    for source, part, start in word_sources(in_refs, pos_ref[0]):
        here = pl.ds(pl.multiple_of(source * SLOTS, SLOTS), SLOTS)
        tail = part[start + SLOTS : start + SLOTS + EXTRA].astype(jnp.float32)
        rows = [jnp.concatenate([tail[2 * p : 2 * p + 1], tail[2 * p + 1 : 2 * p + 2]], axis=1) for p in range(4)]
        total = total + (tail[8:9] + tail[9:10] + tail[10:11])
        data_ref[here, :128] = part[start : start + SLOTS]
        data_ref[here, 128:144] = dot_nt(eye, stack_rows(rows, 16).astype(jnp.bfloat16)).astype(jnp.bfloat16)
    log_total = jnp.log(total)
    for t in range(n // 256):
        cut = slice(256 * t, 256 * t + 256)
        column = to_col(slot_ref[:, cut].astype(jnp.float32)).astype(jnp.int32)
        pick = dot_nn(one_hot(column == iota((256, words * SLOTS), 1)), data_ref[...])
        pick_ref[cut, :] = pick
        weight = to_row(pick[:, 128:129] + pick[:, 129:130] + pick[:, 130:131])
        on_diag = value_of(to_row(pick[:, 131:132]), log_total[:, :1], weight, weight)
        on_diag = on_diag.astype(jnp.bfloat16).astype(jnp.float32)
        stat_ref[:, cut] = stack_rows([weight, on_diag, jnp.broadcast_to(log_total[:, :1], (1, 256))], 8)
    first = pl.multiple_of(ctx * 128, 128)
    near = stat_ref[0:1, pl.ds(first, 128)]
    far = stat_ref[0:1, pl.ds(first + 1024, 128)]
    for t in range(n // 256):
        cut = slice(256 * t, 256 * t + 256)
        pick = pick_ref[cut, :]
        weight = pick[:, 128:129] + pick[:, 129:130] + pick[:, 130:131]
        gap = (iota((256, 128), 1) + ctx * 128 - iota((256, 128), 0) - 256 * t) & 2047
        other = jnp.where((gap >= 1) & (gap <= 1024), near, far)
        out_ref[cut, :] = value_of(pick[:, :128], log_total, weight, other).astype(jnp.bfloat16)


def own_kernel(pos_ref, slot_ref, stat_ref, weight_ref, *refs):
    in_refs, swapped_ref, out_ref = refs[:4], refs[4], refs[5]
    ctx = pos_ref[1]
    n = slot_ref.shape[1]
    out_rows, width = out_ref.shape[0], in_refs[0].shape[1]
    row_log = to_col(weight_ref[0:1])
    for t in range(n // 512):
        cut = slice(512 * t, 512 * t + 512)
        acc = jnp.zeros((out_rows, 512), jnp.float32)
        for r in range(8):
            source = ((ctx >> 1) - (r >> 1) & 3) * 2 + ((ctx ^ r) & 1)
            hot = one_hot(iota((width, 512), 0) + source * width == slot_ref[:, cut])
            step = r // 2
            part = swapped_ref[step * out_rows : (step + 1) * out_rows] if r % 2 else in_refs[step][:out_rows]
            acc += dot_nn(part, hot)
        out_ref[:, cut] = value_of(acc, stat_ref[2:3, cut], row_log, stat_ref[0:1, cut]).astype(jnp.bfloat16)


def move(value, step):
    return lax.ppermute(value, "ctx", [(c, (c + 2 * step) % 8) for c in range(8)])


def swap(value):
    return lax.ppermute(value, "ctx", [(c, c ^ 1) for c in range(8)])


def across(value, step):
    return lax.ppermute(value, "word", [(w, w // 4 * 4 + (w + step) % 4) for w in range(16)])


def along(value, step):
    return lax.ppermute(value, "word", [(w, (w + 4 * step) % 16) for w in range(16)])


def body(counts, row_totals, ctx_totals, samples):
    rows_dev, ctx_dev = counts.shape
    n_word = lax.axis_size("word")
    n_ctx = lax.axis_size("ctx")
    n = samples.shape[0]
    out_rows = rows_dev // n_ctx
    width = 2 * SLOTS
    pos = jnp.stack([lax.axis_index("word"), lax.axis_index("ctx")]).astype(jnp.int32)
    vmem = pl.BlockSpec(memory_space=pltpu.VMEM)
    smem = pl.BlockSpec(memory_space=pltpu.SMEM)
    half = jnp.bfloat16

    hbm = pl.BlockSpec(memory_space=pltpu.HBM)
    *chunks, send, slot = pl.pallas_call(
        select_kernel,
        in_specs=[smem, vmem, hbm],
        out_specs=[vmem] * 7,
        out_shape=[jax.ShapeDtypeStruct((out_rows, width), half)] * 2
        + [jax.ShapeDtypeStruct((2 * out_rows, width), half)] * 3
        + [
            jax.ShapeDtypeStruct((n_ctx, SLOTS + EXTRA, 128), half),
            jax.ShapeDtypeStruct((1, n), jnp.int32),
        ],
        scratch_shapes=[
            pltpu.VMEM((8, SLOTS), jnp.float32),
            pltpu.VMEM((ctx_dev, width), half),
            pltpu.VMEM((rows_dev, width), half),
            pltpu.VMEM((rows_dev, ctx_dev), jnp.int32),
            pltpu.SemaphoreType.DMA((4,)),
        ],
        compiler_params=params(52),
    )(pos, jnp.concatenate([samples, row_totals, ctx_totals]).reshape(1, n + rows_dev + ctx_dev), counts)
    got = lax.all_to_all(send, "ctx", 0, 0, tiled=True)
    send, own_weight = pl.pallas_call(
        block_kernel,
        in_specs=[vmem] * 2,
        out_specs=[vmem, vmem],
        out_shape=[
            jax.ShapeDtypeStruct((SLOTS + EXTRA, 128), half),
            jax.ShapeDtypeStruct((8, 128), jnp.float32),
        ],
        compiler_params=params(16),
    )(row_totals.reshape(1, rows_dev), got)
    line = jnp.concatenate([send] + [across(send, step) for step in (1, -1, 2)], axis=0)
    left, right = along(line, 1), along(line, -1)
    middle = line.shape[0] // 2
    chunks, line = lax.optimization_barrier((chunks, line))
    mine = chunks[:2] + [move(chunks[1 + step], step) for step in (1, 2, 3)]
    lines = [line, left, right, along(left[:middle], 1), along(right[middle:], -1)]
    lines, mine = lax.optimization_barrier((lines, mine))
    part, stat = pl.pallas_call(
        core_kernel,
        in_specs=[smem] + [vmem] * 6,
        out_specs=[vmem, vmem],
        out_shape=[jax.ShapeDtypeStruct((n, 128), half), jax.ShapeDtypeStruct((8, n), jnp.float32)],
        scratch_shapes=[pltpu.VMEM((n_word * SLOTS, 256), half), pltpu.VMEM((n, 256), jnp.float32)],
        compiler_params=params(24),
    )(pos, slot, *lines)
    left, right = move(part, 1), move(part, -1)
    mine, part = lax.optimization_barrier((mine, part))
    swapped = swap(jnp.concatenate([mine[1]] + [value[out_rows:] for value in mine[2:]], axis=0))
    own = pl.pallas_call(
        own_kernel,
        in_specs=[smem] + [vmem] * 8,
        out_specs=vmem,
        out_shape=jax.ShapeDtypeStruct((out_rows, n), half),
        compiler_params=params(16),
        cost_estimate=pl.CostEstimate(flops=4 * out_rows * n * n, bytes_accessed=2 * MEGA, transcendentals=out_rows * n),
    )(pos, slot, stat, own_weight, mine[0], *mine[2:], swapped)
    left, right, own = lax.optimization_barrier((left, right, own))
    parts = [part, left, right, move(left[: n // 2], 1), move(right[n // 2 :], -1)]
    parts = parts + [swap(value) for value in parts]
    return factor(pos, parts, stat, own)


def solution(mesh):
    placed = (P("word", "ctx"), P("word"), P("ctx"), P())
    return jax.shard_map(
        body, mesh=mesh, in_specs=placed, out_specs=P(("word", "ctx"), None), check_vma=False
    )
```

```python
import math

import jax
import jax.numpy as jnp
from jax import lax
from jax.experimental import pallas as pl
from jax.experimental.pallas import tpu as pltpu
from jax.sharding import PartitionSpec as P

SAMPLES = 2048


NEG_LOG = math.log(5.0)


BLOCK = 256
SHIFT = 4.0 * math.sqrt(SAMPLES)
TOLERANCE = 1e-3
ROUNDS = (3, 2, 2, 2, 2, 2, 2, 3)


def dot_nn(left, right):
    return lax.dot_general(left, right, (((1,), (0,)), ((), ())), preferred_element_type=jnp.float32)


def dot_nt(left, right):
    return lax.dot_general(left, right, (((1,), (1,)), ((), ())), preferred_element_type=jnp.float32)


def exact_nt(left, right):
    return lax.dot_general(
        left, right, (((1,), (1,)), ((), ())), precision=lax.Precision.HIGHEST, preferred_element_type=jnp.float32
    )


def direct_factor(stat_ref, own_ref, core_ref, out_ref, tiles_ref, work_ref):
    count = core_ref.shape[1] // BLOCK
    out_rows = own_ref.shape[0]
    row_id = iota((BLOCK, 2 * BLOCK), 0)
    col_id = iota((BLOCK, 2 * BLOCK), 1)
    diag = iota((BLOCK, BLOCK), 0) == iota((BLOCK, BLOCK), 1)

    def span(i):
        return pl.ds(pl.multiple_of(i * BLOCK, BLOCK), BLOCK)

    def place(i, k):
        return i * (i - 1) // 2 + k

    def column(k, carry):
        block = core_ref[span(k), span(k)].astype(jnp.float32)
        block = jnp.where(diag, stat_ref[1:2, span(k)] + SHIFT, block)
        block = lax.fori_loop(
            0, k, lambda m, acc: acc - exact_nt(tiles_ref[place(k, m)], tiles_ref[place(k, m)]), block
        )
        work_ref[:, :BLOCK] = block
        work_ref[:, BLOCK:] = jnp.where(diag, 1.0, 0.0)

        def eliminate(j, carry):
            work = work_ref[...]
            row = jnp.sum(jnp.where(row_id == j, work, 0.0), axis=0, keepdims=True)
            col = jnp.sum(jnp.where(col_id == j, work, 0.0), axis=1, keepdims=True)
            pivot = jnp.sum(jnp.where(col_id[:1] == j, row, 0.0), axis=1, keepdims=True)
            scale = 1.0 / jnp.sqrt(pivot)
            row = row * scale
            work_ref[...] = jnp.where(row_id == j, row, jnp.where(row_id > j, work - (col * scale) * row, work))
            return carry

        lax.fori_loop(0, BLOCK, eliminate, 0)
        inv = work_ref[:, BLOCK:]

        def under(i, carry):
            tile = core_ref[span(i), span(k)].astype(jnp.float32)
            tile = lax.fori_loop(
                0, k, lambda m, acc: acc - exact_nt(tiles_ref[place(i, m)], tiles_ref[place(k, m)]), tile
            )
            tiles_ref[place(i, k)] = exact_nt(tile, inv)
            return carry

        lax.fori_loop(k + 1, count, under, 0)
        mine = own_ref[:, span(k)].astype(jnp.float32)
        mine = lax.fori_loop(
            0, k, lambda m, acc: acc - exact_nt(out_ref[:, span(m)], tiles_ref[place(k, m)]), mine
        )
        out_ref[:, span(k)] = exact_nt(mine, inv)
        return carry

    lax.fori_loop(0, count, column, 0)


def place_parts(refs, ctx, all_ref):
    for source, parts in sources(refs, ctx):
        lanes = pl.ds(pl.multiple_of(source * 128, 128), 128)
        start = 0
        for part in parts:
            all_ref[start : start + part.shape[0], lanes] = part[...]
            start += part.shape[0]


def factor_kernel(pos_ref, stat_ref, own_ref, *refs):
    part_refs, (out_ref, all_ref, core_ref, low_ref, tiles_ref, work_ref) = refs[:10], refs[10:]
    total = core_ref.shape[1]
    middle = total // 2
    half = jnp.bfloat16
    place_parts(part_refs, pos_ref[1], all_ref)
    core_ref[total:] = own_ref[...]
    row_id = iota((BLOCK, BLOCK), 0)
    col_id = iota((BLOCK, BLOCK), 1)
    diag = row_id == col_id
    below = row_id > col_id
    above = row_id < col_id
    eye = one_hot(diag)
    zero = jnp.zeros((BLOCK, BLOCK), half)

    def turned(tile):
        return dot_nt(eye, tile).astype(half)

    count = middle // BLOCK
    for i in range(count):
        for side in (0, middle):
            here = slice(side + i * BLOCK, side + (i + 1) * BLOCK)
            for j in range(i):
                core_ref[here, side + j * BLOCK : side + (j + 1) * BLOCK] = turned(
                    all_ref[side + j * BLOCK : side + (j + 1) * BLOCK, i * BLOCK : (i + 1) * BLOCK]
                )
            upper = jnp.where(above, all_ref[here, i * BLOCK : (i + 1) * BLOCK], zero)
            core_ref[here, here] = upper + turned(upper)
        here = slice(middle + i * BLOCK, middle + (i + 1) * BLOCK)
        for j in range(count):
            cols = slice(j * BLOCK, (j + 1) * BLOCK)
            if i > j:
                tile = all_ref[here, cols]
            else:
                tile = turned(all_ref[cols, i * BLOCK : (i + 1) * BLOCK])
            if i == j:
                tile = jnp.where(above, tile, all_ref[here, cols])
            core_ref[here, cols] = tile

    weight = jnp.where(below, 1.0, jnp.where(diag, 0.5, 0.0))
    worst = jnp.zeros((1, 1), jnp.float32)
    for k in range(total // BLOCK):
        lo, hi = k * BLOCK, (k + 1) * BLOCK
        block = core_ref[lo:hi, lo:hi].astype(jnp.float32)
        block = jnp.where(diag, stat_ref[1:2, lo:hi] + SHIFT, block)
        if k:
            past = dot_nt(low_ref[lo:, :lo], low_ref[lo:hi, :lo])
            block = block - past[:BLOCK]
        on_diag = jnp.where(diag, block, 0.0)
        scale_col = lax.rsqrt(jnp.sum(on_diag, axis=1, keepdims=True))
        scale_row = lax.rsqrt(jnp.sum(on_diag, axis=0, keepdims=True))
        off = jnp.where(diag, 0.0, block * scale_col * scale_row)
        step = off * weight
        inv = -step
        for _ in range(ROUNDS[k]):
            step_half = step.astype(half)
            inner = dot_nn(step_half, off.astype(half))
            off = dot_nt((inner + step - off).astype(half), step_half) - inner
            step = off * weight
            inv = inv - step - dot_nn(step.astype(half), inv.astype(half))
        worst = jnp.maximum(worst, jnp.sum(step * step, keepdims=True))
        inv_half = inv.astype(half)
        under = core_ref[hi:, lo:hi].astype(jnp.float32)
        if k:
            under = under - past[BLOCK:]
        under = under * scale_row
        under = under + dot_nt(under.astype(half), inv_half)
        low_ref[hi:, lo:hi] = under.astype(half)
        out_ref[:, lo:hi] = under[total - hi :]

    @pl.when(jnp.logical_not(worst[0, 0] < TOLERANCE))
    def _():
        direct_factor(stat_ref, own_ref, core_ref, out_ref, tiles_ref, work_ref)


def factor(pos, parts, stat, own):
    out_rows, total = own.shape
    count = total // BLOCK
    vmem = pl.BlockSpec(memory_space=pltpu.VMEM)
    smem = pl.BlockSpec(memory_space=pltpu.SMEM)
    return pl.pallas_call(
        factor_kernel,
        out_shape=jax.ShapeDtypeStruct((out_rows, total), jnp.float32),
        in_specs=[smem] + [vmem] * 12,
        out_specs=vmem,
        scratch_shapes=[
            pltpu.VMEM((total, total // 2), jnp.bfloat16),
            pltpu.VMEM((total + out_rows, total), jnp.bfloat16),
            pltpu.VMEM((total + out_rows, total), jnp.bfloat16),
            pltpu.VMEM((count * (count - 1) // 2, BLOCK, BLOCK), jnp.float32),
            pltpu.VMEM((BLOCK, 2 * BLOCK), jnp.float32),
        ],
        compiler_params=params(40),
    )(pos, stat, own, *parts)


SLOTS = 256
EXTRA = 16
MEGA = 1024 * 1024


def params(limit=48):
    return pltpu.CompilerParams(vmem_limit_bytes=limit * MEGA)


def iota(shape, dim):
    return lax.broadcasted_iota(jnp.int32, shape, dim)


def to_col(row):
    n = row.shape[1]
    square = iota((n, n), 0) == iota((n, n), 1)
    return jnp.sum(jnp.where(square, jnp.broadcast_to(row, (n, n)), 0.0), axis=1, keepdims=True)


def to_row(col):
    n = col.shape[0]
    square = iota((n, n), 0) == iota((n, n), 1)
    return jnp.sum(jnp.where(square, jnp.broadcast_to(col, (n, n)), 0.0), axis=0, keepdims=True)


def stack_rows(rows, height):
    width = rows[0].shape[1]
    index = iota((height, width), 0)
    out = jnp.zeros((height, width), jnp.float32)
    for r, row in enumerate(rows):
        out = jnp.where(index == r, jnp.broadcast_to(row, (height, width)), out)
    return out


def one_hot(mask):
    return jnp.where(mask, 1.0, 0.0).astype(jnp.bfloat16)


def pieces(value):
    high = value.astype(jnp.bfloat16).astype(jnp.float32)
    rest = value - high
    middle = rest.astype(jnp.bfloat16).astype(jnp.float32)
    return [high, middle, rest - middle]


def select_kernel(pos_ref, small_ref, counts_hbm, *refs):
    chunk_refs, (send_ref, slot_ref, index_ref, hot_ref, picked_ref) = refs[:5], refs[5:10]
    counts_ref, sems = refs[10:]
    word, ctx = pos_ref[0], pos_ref[1]
    n = slot_ref.shape[1]
    width = hot_ref.shape[1]
    share = chunk_refs[0].shape[0]
    rows = 2 * share
    steps = counts_ref.shape[0] // rows
    copies = []
    for g in range(steps):
        cut = slice(g * rows, (g + 1) * rows)
        copies.append(pltpu.make_async_copy(counts_hbm.at[cut], counts_ref.at[cut], sems.at[g]))
        copies[g].start()

    sample = small_ref[:, :n]
    block = sample >> 10
    member = jnp.where(iota((16, n), 0) == block, 1.0, 0.0)
    before = one_hot(iota((256, 256), 0) < iota((256, 256), 1))
    count = jnp.zeros((16, 1), jnp.float32)
    k = iota((1, n), 1)
    local = sample & 2047
    vals = stack_rows(
        [v.astype(jnp.float32) for v in (local >> 8, local & 255, local * 0 + 1, k >> 8, k & 255, (local & 1023) >> 8)],
        8,
    ).astype(jnp.bfloat16)
    by_ctx = jnp.zeros((8, width), jnp.float32)
    by_word = jnp.zeros((8, SLOTS), jnp.float32)
    for t in range(n // 256):
        cut = slice(256 * t, 256 * t + 256)
        mine = member[:, cut]
        rank = dot_nn(mine.astype(jnp.bfloat16), before) + count
        count = count + jnp.sum(mine, axis=1, keepdims=True)
        slot = block[:, cut].astype(jnp.float32) * SLOTS + jnp.sum(mine * rank, axis=0, keepdims=True)
        slot_ref[:, cut] = slot.astype(jnp.int32)
        column = to_col(slot).astype(jnp.int32)
        by_ctx += dot_nn(vals[:, cut], one_hot(column - ctx * width == iota((256, width), 1)))
        by_word += dot_nn(vals[:, cut], one_hot(column - word * SLOTS == iota((256, SLOTS), 1)))
    col = jnp.where(by_ctx[2:3] > 0, by_ctx[0:1] * 256 + by_ctx[1:2], -1.0).astype(jnp.int32)
    for t in range(hot_ref.shape[0] // 256):
        hot_ref[256 * t : 256 * t + 256] = one_hot(iota((256, width), 0) + 256 * t == col)
    row = jnp.where(by_word[2:3] > 0, by_word[5:6] * 256 + by_word[1:2], -1.0)
    index_ref[...] = stack_rows([row, by_word[3:4] * 256 + by_word[4:5]], 8)

    for g in range(steps):
        if g % 2 == 0:
            copies[g].wait()
            copies[g + 1].wait()
            cut = slice(g * rows, (g + 2) * rows)
            pair = counts_ref[cut].astype(jnp.float32).astype(jnp.bfloat16)
            pair = dot_nn(pair, hot_ref[...]).astype(jnp.bfloat16)
            picked_ref[cut] = pair
        chunk = pair[g % 2 * rows : (g % 2 + 1) * rows]
        odd = (ctx & 1) == 1
        same = jnp.where(odd, chunk[share:], chunk[:share])
        other = jnp.where(odd, chunk[:share], chunk[share:])
        for r in range(steps):

            @pl.when((g - (ctx >> 1) & 3) == r)
            def _(r=r, same=same, other=other):
                if r == 0:
                    chunk_refs[0][...] = same
                    chunk_refs[1][...] = other
                else:
                    chunk_refs[1 + r][:share] = same
                    chunk_refs[1 + r][share:] = other

    total_rows = picked_ref.shape[0]
    row_hot = one_hot(to_col(index_ref[0:1]).astype(jnp.int32) == iota((SLOTS, total_rows), 1))
    picked = dot_nn(row_hot, picked_ref[...])
    tile = jnp.where((word & 1) == 1, picked[:, SLOTS:], picked[:, :SLOTS])
    square = iota((SLOTS, SLOTS), 0) == iota((SLOTS, SLOTS), 1)
    own_diag = jnp.sum(jnp.where(square, tile, 0.0), axis=0, keepdims=True)
    here = small_ref[:, pl.ds(pl.multiple_of(n + total_rows + (word & 1) * total_rows, total_rows), total_rows)]
    weight = 0.5 * (jnp.log(small_ref[:, n : n + total_rows].astype(jnp.float32)) + jnp.log(here.astype(jnp.float32)))
    weight_parts = pieces(weight)
    slot_weight = dot_nt(stack_rows(weight_parts, 16).astype(jnp.bfloat16), row_hot)
    parts = []
    for p in range(3):
        parts += [slot_weight[p : p + 1, :128], slot_weight[p : p + 1, 128:]]
    parts += [own_diag[:, :128], own_diag[:, 128:]]
    holder = ctx == word >> 1
    full = dot_nn(
        picked.astype(jnp.bfloat16), one_hot(iota((width, n), 0) + ctx * width == slot_ref[...])
    )
    k_col = to_col(index_ref[1:2]).astype(jnp.int32)
    gap = (iota((SLOTS, n // 2), 1) - k_col) & (n - 1)
    head = jnp.where((gap >= 1) & (gap <= n // 2), full[:, : n // 2], full[:, n // 2 :]).astype(jnp.bfloat16)
    for c in range(8):
        lanes = slice(128 * c, 128 * c + 128)
        tail = stack_rows(parts + [p[:, lanes] for p in weight_parts], EXTRA)
        send_ref[c, :SLOTS] = head[:, lanes]
        send_ref[c, SLOTS:] = jnp.where(holder, tail, 0.0).astype(jnp.bfloat16)


def sources(refs, ctx):
    z, core = ctx >> 1, ctx & 1
    out = []
    for half in (0, 1):
        own, left, right, top, bottom = refs[5 * half : 5 * half + 5]
        for step, parts in ((0, (own,)), (3, (left,)), (1, (right,)), (2, (top, bottom))):
            out.append((((z + step) & 3) * 2 + (core ^ half), parts))
    return out


def block_kernel(totals_ref, got_ref, send_ref, own_ref):
    got = got_ref[0].astype(jnp.float32)
    for c in range(1, got_ref.shape[0]):
        got = got + got_ref[c].astype(jnp.float32)
    tail = got[SLOTS:]
    own_ref[...] = jnp.broadcast_to(tail[8:9] + tail[9:10] + tail[10:11], own_ref.shape)
    total = pieces(jnp.sum(totals_ref[...].astype(jnp.float32), axis=1, keepdims=True))
    row = iota(tail.shape, 0)
    for p in range(3):
        tail = jnp.where(row == 8 + p, jnp.broadcast_to(total[p], tail.shape), tail)
    send_ref[:SLOTS] = got[:SLOTS].astype(jnp.bfloat16)
    send_ref[SLOTS:] = tail.astype(jnp.bfloat16)


def value_of(count, log_total, row_log, col_log):
    value = jnp.log(jnp.maximum(count, 1.0)) + log_total - row_log - col_log - NEG_LOG
    return jnp.where(count > 0, jnp.maximum(value, 0.0), 0.0)


def word_sources(refs, word):
    y, x = word >> 2, word & 3
    own, left, right, top, bottom = refs
    for step, parts in ((0, (own,)), (3, (left,)), (1, (right,)), (2, (top, bottom))):
        for i, across in enumerate((0, 3, 1, 2)):
            part, place = (parts[0], i) if len(parts) == 1 else (parts[i // 2], i % 2)
            yield ((y + step) & 3) * 4 + ((x + across) & 3), part, place * (SLOTS + EXTRA)


def core_kernel(pos_ref, slot_ref, *refs):
    in_refs, (out_ref, stat_ref, data_ref, pick_ref) = refs[:5], refs[5:]
    ctx = pos_ref[1]
    n = slot_ref.shape[1]
    words = data_ref.shape[0] // SLOTS
    eye = one_hot(iota((SLOTS, SLOTS), 0) == iota((SLOTS, SLOTS), 1))
    data_ref[:, 128:] = jnp.zeros((words * SLOTS, 128), jnp.bfloat16)
    total = jnp.zeros((1, 128), jnp.float32)
    for source, part, start in word_sources(in_refs, pos_ref[0]):
        here = pl.ds(pl.multiple_of(source * SLOTS, SLOTS), SLOTS)
        tail = part[start + SLOTS : start + SLOTS + EXTRA].astype(jnp.float32)
        rows = [jnp.concatenate([tail[2 * p : 2 * p + 1], tail[2 * p + 1 : 2 * p + 2]], axis=1) for p in range(4)]
        total = total + (tail[8:9] + tail[9:10] + tail[10:11])
        data_ref[here, :128] = part[start : start + SLOTS]
        data_ref[here, 128:144] = dot_nt(eye, stack_rows(rows, 16).astype(jnp.bfloat16)).astype(jnp.bfloat16)
    log_total = jnp.log(total)
    for t in range(n // 256):
        cut = slice(256 * t, 256 * t + 256)
        column = to_col(slot_ref[:, cut].astype(jnp.float32)).astype(jnp.int32)
        pick = dot_nn(one_hot(column == iota((256, words * SLOTS), 1)), data_ref[...])
        pick_ref[cut, :] = pick
        weight = to_row(pick[:, 128:129] + pick[:, 129:130] + pick[:, 130:131])
        on_diag = value_of(to_row(pick[:, 131:132]), log_total[:, :1], weight, weight)
        on_diag = on_diag.astype(jnp.bfloat16).astype(jnp.float32)
        stat_ref[:, cut] = stack_rows([weight, on_diag, jnp.broadcast_to(log_total[:, :1], (1, 256))], 8)
    first = pl.multiple_of(ctx * 128, 128)
    near = stat_ref[0:1, pl.ds(first, 128)]
    far = stat_ref[0:1, pl.ds(first + 1024, 128)]
    for t in range(n // 256):
        cut = slice(256 * t, 256 * t + 256)
        pick = pick_ref[cut, :]
        weight = pick[:, 128:129] + pick[:, 129:130] + pick[:, 130:131]
        gap = (iota((256, 128), 1) + ctx * 128 - iota((256, 128), 0) - 256 * t) & 2047
        other = jnp.where((gap >= 1) & (gap <= 1024), near, far)
        out_ref[cut, :] = value_of(pick[:, :128], log_total, weight, other).astype(jnp.bfloat16)


def own_kernel(pos_ref, slot_ref, stat_ref, weight_ref, *refs):
    in_refs, swapped_ref, out_ref = refs[:4], refs[4], refs[5]
    ctx = pos_ref[1]
    n = slot_ref.shape[1]
    out_rows, width = out_ref.shape[0], in_refs[0].shape[1]
    row_log = to_col(weight_ref[0:1])
    for t in range(n // 512):
        cut = slice(512 * t, 512 * t + 512)
        acc = jnp.zeros((out_rows, 512), jnp.float32)
        for r in range(8):
            source = ((ctx >> 1) - (r >> 1) & 3) * 2 + ((ctx ^ r) & 1)
            hot = one_hot(iota((width, 512), 0) + source * width == slot_ref[:, cut])
            step = r // 2
            part = swapped_ref[step * out_rows : (step + 1) * out_rows] if r % 2 else in_refs[step][:out_rows]
            acc += dot_nn(part, hot)
        out_ref[:, cut] = value_of(acc, stat_ref[2:3, cut], row_log, stat_ref[0:1, cut]).astype(jnp.bfloat16)


def move(value, step):
    return lax.ppermute(value, "ctx", [(c, (c + 2 * step) % 8) for c in range(8)])


def swap(value):
    return lax.ppermute(value, "ctx", [(c, c ^ 1) for c in range(8)])


def across(value, step):
    return lax.ppermute(value, "word", [(w, w // 4 * 4 + (w + step) % 4) for w in range(16)])


def along(value, step):
    return lax.ppermute(value, "word", [(w, (w + 4 * step) % 16) for w in range(16)])


def body(counts, row_totals, ctx_totals, samples):
    rows_dev, ctx_dev = counts.shape
    n_word = lax.axis_size("word")
    n_ctx = lax.axis_size("ctx")
    n = samples.shape[0]
    out_rows = rows_dev // n_ctx
    width = 2 * SLOTS
    pos = jnp.stack([lax.axis_index("word"), lax.axis_index("ctx")]).astype(jnp.int32)
    vmem = pl.BlockSpec(memory_space=pltpu.VMEM)
    smem = pl.BlockSpec(memory_space=pltpu.SMEM)
    half = jnp.bfloat16

    hbm = pl.BlockSpec(memory_space=pltpu.HBM)
    *chunks, send, slot = pl.pallas_call(
        select_kernel,
        in_specs=[smem, vmem, hbm],
        out_specs=[vmem] * 7,
        out_shape=[jax.ShapeDtypeStruct((out_rows, width), half)] * 2
        + [jax.ShapeDtypeStruct((2 * out_rows, width), half)] * 3
        + [
            jax.ShapeDtypeStruct((n_ctx, SLOTS + EXTRA, 128), half),
            jax.ShapeDtypeStruct((1, n), jnp.int32),
        ],
        scratch_shapes=[
            pltpu.VMEM((8, SLOTS), jnp.float32),
            pltpu.VMEM((ctx_dev, width), half),
            pltpu.VMEM((rows_dev, width), half),
            pltpu.VMEM((rows_dev, ctx_dev), jnp.int32),
            pltpu.SemaphoreType.DMA((4,)),
        ],
        compiler_params=params(52),
    )(pos, jnp.concatenate([samples, row_totals, ctx_totals]).reshape(1, n + rows_dev + ctx_dev), counts)
    got = lax.all_to_all(send, "ctx", 0, 0, tiled=True)
    send, own_weight = pl.pallas_call(
        block_kernel,
        in_specs=[vmem] * 2,
        out_specs=[vmem, vmem],
        out_shape=[
            jax.ShapeDtypeStruct((SLOTS + EXTRA, 128), half),
            jax.ShapeDtypeStruct((8, 128), jnp.float32),
        ],
        compiler_params=params(16),
    )(row_totals.reshape(1, rows_dev), got)
    line = jnp.concatenate([send] + [across(send, step) for step in (1, -1, 2)], axis=0)
    left, right = along(line, 1), along(line, -1)
    middle = line.shape[0] // 2
    chunks, line = lax.optimization_barrier((chunks, line))
    mine = chunks[:2] + [move(chunks[1 + step], step) for step in (1, 2, 3)]
    lines = [line, left, right, along(left[:middle], 1), along(right[middle:], -1)]
    lines, mine = lax.optimization_barrier((lines, mine))
    part, stat = pl.pallas_call(
        core_kernel,
        in_specs=[smem] + [vmem] * 6,
        out_specs=[vmem, vmem],
        out_shape=[jax.ShapeDtypeStruct((n, 128), half), jax.ShapeDtypeStruct((8, n), jnp.float32)],
        scratch_shapes=[pltpu.VMEM((n_word * SLOTS, 256), half), pltpu.VMEM((n, 256), jnp.float32)],
        compiler_params=params(24),
    )(pos, slot, *lines)
    left, right = move(part, 1), move(part, -1)
    mine, part = lax.optimization_barrier((mine, part))
    swapped = swap(jnp.concatenate([mine[1]] + [value[out_rows:] for value in mine[2:]], axis=0))
    own = pl.pallas_call(
        own_kernel,
        in_specs=[smem] + [vmem] * 8,
        out_specs=vmem,
        out_shape=jax.ShapeDtypeStruct((out_rows, n), half),
        compiler_params=params(16),
        cost_estimate=pl.CostEstimate(flops=4 * out_rows * n * n, bytes_accessed=2 * MEGA, transcendentals=out_rows * n),
    )(pos, slot, stat, own_weight, mine[0], *mine[2:], swapped)
    left, right, own = lax.optimization_barrier((left, right, own))
    parts = [part, left, right, move(left[: n // 2], 1), move(right[n // 2 :], -1)]
    parts = parts + [swap(value) for value in parts]
    return factor(pos, parts, stat, own)


def solution(mesh):
    placed = (P("word", "ctx"), P("word"), P("ctx"), P())
    return jax.shard_map(
        body, mesh=mesh, in_specs=placed, out_specs=P(("word", "ctx"), None), check_vma=False
    )
```
